1024 devices in a mesh: dp: 4 (over x_hi, core), mp: 256 (over z, x_lo, y).
Axes of the slice: x: 4 (x_hi: 2, x_lo: 2; x = x_hi * 2 + x_lo), y: 8, z: 16, core: 2. Of those that a mesh axis runs over, the one named last changes fastest.
Arguments:
- block_input: bfloat16 [768, 6144], P('dp'), may hold values from -6 to 6
- grad_out: bfloat16 [768, 6144], P('dp'), may hold values from -6 to 6
- ln_gain: float32 [6144], replicated, may hold values from 0.1 to 1.9
- w_in: bfloat16 [6144, 24576], P(None, 'mp'), may hold values from -0.078125 to 0.078125
- w_out: bfloat16 [24576, 6144], P('mp'), may hold values from -0.0390625 to 0.0390625
Outputs:
- grad_input: bfloat16 [768, 6144], P('dp', 'mp')
- grad_w_in: float32 [6144, 24576], P('dp', 'mp')
- grad_w_out: float32 [24576, 6144], P('mp', 'dp')
The draws below stay inside these ranges and needn't reach their ends.
All inputs are finite; a program needn't handle non-finite values.
Results may differ from the reference program's by a relative error of at most 0.0055.
Values may be sent and summed in bfloat16 or wider, within the bound.
A program may use at most 64 MiB of HBM per device.

```python
import jax
import jax.numpy as jnp
from jax import lax

D = 6144
FF = 24576
TOK = 768


def spiked(entries, key, source, target, blocks, factor):
    def block_of(position):
        return (jnp.arange(entries.shape[position]) // (entries.shape[position] // blocks)).reshape((-1,) + (1,) * (entries.ndim - 1 - position))

    one_side = jax.random.permutation(key, blocks)[block_of(target)]
    far = (block_of(target) + blocks // 2) % blocks
    return jnp.where((block_of(source) == one_side) | (block_of(source) == far), factor * entries, entries)


def levels(own_key, extent, cuts, low, top_value):
    loudness = 1.0
    for dim, blocks in cuts:
        draws = jax.random.uniform(jax.random.fold_in(jax.random.fold_in(own_key, 6), dim), (blocks,), jnp.float32, low / len(cuts), top_value / len(cuts))
        loudness = loudness * jnp.repeat(jnp.exp(draws), extent[dim] // blocks).reshape((-1,) + (1,) * (len(extent) - 1 - dim))
    return loudness


def noise(own_key, shape, deviation, bound, shards=(), kind=jnp.bfloat16):
    result = deviation * jax.random.normal(own_key, shape, jnp.float32)
    if shards:
        result = result * levels(own_key, shape, shards, -0.22, 0.18)
    return jnp.clip(result, -bound, bound).astype(kind)


def heavy_noise(key, extent, width, most, split, heavy, held_as=jnp.bfloat16):
    result = width * jax.random.normal(key, extent, jnp.float32)
    if split:
        result = result * levels(key, extent, split, -0.22, 0.18)
    return jnp.clip(spiked(result, jax.random.fold_in(key, 3), *heavy), -most, most).astype(held_as)


def setup_inputs(seed: int = 0) -> dict:
    key_list = jax.random.split(jax.random.key(seed), 6)
    block_input = noise(key_list[0], (TOK, D), 1.0, 6.0, ((0, 4),))
    grad_out = heavy_noise(key_list[1], (TOK, D), 1.0, 6.0, ((0, 4),), (0, 1, 4, 2.0))
    ln_gain = jnp.clip(1.0 + 0.18 * jax.random.normal(key_list[2], (D,), jnp.float32), 0.1, 1.9)
    w_in = noise(key_list[3], (D, FF), D ** -0.5, 0.078125, ((1, 256),))
    w_out = noise(key_list[4], (FF, D), FF ** -0.5, 0.0390625, ((0, 256),))
    return {"block_input": block_input, "grad_out": grad_out, "ln_gain": ln_gain, "w_in": w_in, "w_out": w_out}


def gelu_slope(pre_gelu):
    normal_cdf = 0.5 * (1.0 + lax.erf(pre_gelu * 0.7071067811865476))
    return normal_cdf + pre_gelu * jnp.exp(-0.5 * pre_gelu * pre_gelu) * 0.3989422804014327

def reference(block_input, grad_out, ln_gain, w_in, w_out):
    input_float = block_input.astype(jnp.float32)
    centred = input_float - lax.optimization_barrier(jnp.mean(input_float, axis=1, keepdims=True))
    inv_std = lax.rsqrt(lax.optimization_barrier(jnp.mean(centred * centred, axis=1, keepdims=True)) + 1e-06)
    normed = centred * inv_std
    gain_normed = (normed * ln_gain).astype(jnp.bfloat16)
    pre_gelu = jnp.dot(gain_normed, w_in, preferred_element_type=jnp.float32)
    activation = jax.nn.gelu(pre_gelu, approximate=False).astype(jnp.bfloat16)
    grad_act = lax.dot_general(grad_out, w_out, (((1,), (1,)), ((), ())), preferred_element_type=jnp.float32)
    grad_pre = (grad_act * gelu_slope(pre_gelu)).astype(jnp.bfloat16)
    grad_w_out = lax.dot_general(activation, grad_out, (((0,), (0,)), ((), ())), preferred_element_type=jnp.float32)
    grad_w_in = lax.dot_general(gain_normed, grad_pre, (((0,), (0,)), ((), ())), preferred_element_type=jnp.float32)
    grad_gained = lax.dot_general(grad_pre, w_in, (((1,), (1,)), ((), ())), preferred_element_type=jnp.float32)
    grad_normed = grad_gained * ln_gain
    mean_one = lax.optimization_barrier(jnp.mean(grad_normed, axis=1, keepdims=True))
    mean_two = lax.optimization_barrier(jnp.mean(grad_normed * normed, axis=1, keepdims=True))
    grad_input = (grad_out.astype(jnp.float32) + inv_std * (grad_normed - mean_one - normed * mean_two)).astype(jnp.bfloat16)
    return (grad_input, grad_w_in, grad_w_out)
```

```python
import jax
import jax.numpy as jnp
from jax import lax
from jax.experimental import pallas as pl
from jax.experimental.pallas import tpu as pltpu
from jax.sharding import PartitionSpec as P

F32 = jnp.float32
BF16 = jnp.bfloat16
D = 6144
TOK = 192
HID = 96
LANE = 128
NY = 8
NZ = 16
YCOL = D // NY
XCOL = YCOL // 2
PIECE = XCOL // NZ
QUART = D // 4
XROWS = 48


def contract_last(left, right):
    return lax.dot_general(left, right, (((1,), (1,)), ((), ())), preferred_element_type=F32)


def remote(src, dst, send, recv, dp, mp):
    return pltpu.make_async_remote_copy(
        src_ref=src,
        dst_ref=dst,
        send_sem=send,
        recv_sem=recv,
        device_id=(dp, mp),
        device_id_type=pl.DeviceIdType.MESH,
    )


def hi_lo(value):
    high = value.astype(BF16).astype(F32)
    return high, (value - high).astype(BF16).astype(F32)


def kernel(
    x_hbm, go_hbm, gain_ref, win_hbm, wout_hbm,
    gi_ref, gwin_ref, gwout_ref,
    x_v, go_v, g_v, win_v, wout_v, wg, gpg, gain3, pre_s, ga_s, u_s, stat_s, tr_s, gp_t, act_t,
    pair_send, pair_recv, xh_send, xh_recv, gg_s, gg_t, xl_send, xl_recv, st_t, xst_send, xst_recv,
    z_send, z_recv, last_send, last_recv,
    x_sem, load_sem, a_send, a_recv, f_send, f_recv, y_send, y_recv, p_send, p_recv,
    h_send, h_recv, l_send, l_recv, s_send, s_recv, zs_sem, zr_sem, e_send, e_recv,
):
    dp = lax.axis_index("dp")
    mp = lax.axis_index("mp")
    xh, core = dp // 2, dp % 2
    z, xl, y = mp // 16, (mp // 8) % 2, mp % 8
    pair = 2 * xh + (1 - core)
    far = 2 * (1 - xh) + core
    xl_mp = z * 16 + (1 - xl) * 8 + y
    to_mp = (2 * y + xl) * 16 + (z // 8) * 8 + z % 8
    from_mp = (8 * xl + y) * 16 + (z % 2) * 8 + z // 2

    def y_mp(other):
        return z * 16 + xl * 8 + other

    def z_mp(other):
        return other * 16 + xl * 8 + y

    x_loads = [
        pltpu.make_async_copy(
            x_hbm.at[pl.ds(i * XROWS, XROWS)], x_v.at[pl.ds(i * XROWS, XROWS)], x_sem.at[i]
        )
        for i in range(TOK // XROWS)
    ]
    win_load = pltpu.make_async_copy(win_hbm, win_v.at[pl.ds(0, HID)], load_sem.at[0])
    wout_load = pltpu.make_async_copy(wout_hbm, wout_v.at[pl.ds(0, HID)], load_sem.at[1])
    go_load = pltpu.make_async_copy(go_hbm, go_v, load_sem.at[2])
    own_cols = pl.ds(pl.multiple_of(y * YCOL, YCOL), YCOL)
    own_load = pltpu.make_async_copy(
        win_hbm.at[:, own_cols],
        wg.at[pl.ds(pl.multiple_of(y * LANE, LANE), HID)],
        load_sem.at[3],
    )
    for load in x_loads:
        load.start()
    win_load.start()
    wout_load.start()
    go_load.start()
    own_load.start()

    barrier = pltpu.get_barrier_semaphore()

    def greet(to_dp, to_mp_):
        pl.semaphore_signal(
            barrier, inc=1, device_id=(to_dp, to_mp_), device_id_type=pl.DeviceIdType.MESH
        )

    @pl.loop(1, NY)
    def _(d):
        greet(dp, y_mp((y + d) % NY))

    @pl.loop(1, NZ)
    def _(d):
        greet(dp, z_mp((z + d) % NZ))

    greet(pair, mp)
    greet(far, mp)
    greet(dp, xl_mp)
    moves = to_mp != mp

    @pl.when(moves)
    def _():
        greet(dp, to_mp)
        greet(dp, from_mp)

    pl.semaphore_wait(barrier, NY - 1 + NZ - 1 + 3 + jnp.where(moves, 2, 0))

    def block_copy(d):
        other = (y + d) % NY
        return remote(
            win_hbm.at[pl.ds(pl.multiple_of(core * 48, 16), 48), pl.ds(pl.multiple_of(other * YCOL, YCOL), YCOL)],
            wg.at[pl.ds(pl.multiple_of(y * LANE + core * 48, 16), 48)],
            a_send.at[d], a_recv.at[d], dp, y_mp(other),
        )

    def block_landed(d):
        source = (y + NY - d) % NY
        return wg.at[pl.ds(pl.multiple_of(source * LANE + core * 48, 16), 48)]

    def block_arrival(d):
        landed = block_landed(d)
        return remote(landed, landed, a_send.at[d], a_recv.at[d], dp, y_mp((y + d) % NY))

    def forward(d):
        landed = block_landed(d)
        return remote(landed, landed, f_send.at[d], f_recv.at[d], pair, mp)

    def forward_arrival(d):
        source = (y + NY - d) % NY
        landed = wg.at[pl.ds(pl.multiple_of(source * LANE + (1 - core) * 48, 16), 48)]
        return remote(landed, landed, f_send.at[d], f_recv.at[d], pair, mp)

    @pl.loop(1, NY)
    def _(d):
        block_copy(d).start()

    for i in range(NY):
        wg[i * LANE + HID : (i + 1) * LANE, :] = jnp.zeros((LANE - HID, YCOL), BF16)
    win_v[HID:, :] = jnp.zeros((LANE - HID, D), BF16)
    wout_v[HID:, :] = jnp.zeros((LANE - HID, D), BF16)

    lane = lax.broadcasted_iota(jnp.int32, (16, LANE), 1)
    for i in range(TOK // XROWS):
        x_loads[i].wait()

        @pl.loop(0, XROWS // 16)
        def _(t):
            rows = pl.ds(pl.multiple_of(i * XROWS + t * 16, 16), 16)
            tile = x_v[rows, :].astype(F32)
            mean = jnp.sum(tile, axis=1, keepdims=True) * (1.0 / D)
            centred = tile - mean
            inv = lax.rsqrt(jnp.sum(centred * centred, axis=1, keepdims=True) * (1.0 / D) + 1e-06)
            g_v[rows, :] = (centred * inv * gain_ref[...]).astype(BF16)
            stat_s[rows, :] = jnp.where(lane < 64, mean, inv)

    gain = gain_ref[...]
    g_hi = gain.astype(BF16).astype(F32)
    g_mid = (gain - g_hi).astype(BF16).astype(F32)
    g_low = gain - g_hi - g_mid
    row = lax.broadcasted_iota(jnp.int32, (16, D), 0)
    gain3[...] = jnp.where(
        row == 0, g_hi, jnp.where(row == 1, g_mid, jnp.where(row == 2, g_low, 0.0))
    ).astype(BF16)

    win_load.wait()
    wout_load.wait()
    go_load.wait()
    pre_s[...] = jnp.zeros_like(pre_s)
    ga_s[...] = jnp.zeros_like(ga_s)
    u_s[...] = jnp.zeros_like(u_s)

    @pl.loop(0, 4)
    def _(k):
        part = pl.ds(pl.multiple_of(k * 1536, 1536), 1536)
        w_part = win_v[:, part]
        pre_s[...] += contract_last(g_v[:, part], w_part)
        u_s[...] += contract_last(gain3[:, part], w_part)
        ga_s[...] += contract_last(go_v[:, part], wout_v[:, part])

    pre = pre_s[...]
    cdf = 0.5 * (1.0 + lax.erf(pre * 0.7071067811865476))
    act = (pre * cdf).astype(BF16).astype(F32)
    slope = cdf + pre * jnp.exp(-0.5 * pre * pre) * 0.3989422804014327
    gp = (ga_s[...] * slope).astype(BF16).astype(F32)
    u_row = jnp.sum(u_s[...], axis=0, keepdims=True)
    one_hi, one_lo = hi_lo(jnp.sum(gp * u_row, axis=1, keepdims=True))
    two_hi, two_lo = hi_lo(jnp.sum(gp * pre, axis=1, keepdims=True))
    lanes = lax.broadcasted_iota(jnp.int32, (TOK, LANE), 1)
    tail = jnp.where(lanes == HID, one_hi, 0.0)
    tail = jnp.where(lanes == HID + 1, one_lo, tail)
    tail = jnp.where(lanes == HID + 2, two_hi, tail)
    tail = jnp.where(lanes == HID + 3, two_lo, tail)
    own_block = pl.ds(pl.multiple_of(y * LANE, LANE), LANE)
    gpg[:, own_block] = (gp + tail).astype(BF16)

    def gather_copy(d):
        mine = gpg.at[:, own_block]
        return remote(mine, mine, y_send.at[d], y_recv.at[d], dp, y_mp((y + d) % NY))

    def gather_arrival(d):
        source = (y + NY - d) % NY
        landed = gpg.at[:, pl.ds(pl.multiple_of(source * LANE, LANE), LANE)]
        return remote(landed, landed, y_send.at[d], y_recv.at[d], dp, y_mp((y + d) % NY))

    @pl.loop(1, NY)
    def _(d):
        gather_copy(d).start()

    tr_s[TOK:, :] = jnp.zeros((256 - TOK, LANE), F32)
    for values, target in ((gp, gp_t), (act, act_t)):
        tr_s[:TOK, :] = values
        for b in range(2):
            target[:, b * 128 : (b + 1) * 128] = tr_s[b * 128 : (b + 1) * 128, :].T.astype(BF16)
    sides = ((gp_t, g_v, gwin_ref), (act_t, go_v, gwout_ref))

    def product(side, quarter, t):
        left, right, _ = sides[side]
        cols = pl.ds(pl.multiple_of(quarter * QUART + t * 768, 128), 768)
        return jnp.dot(left[:HID, :TOK], right[:, cols], preferred_element_type=F32)

    def pair_copy(r):
        return remote(pair_send.at[r], pair_recv.at[r], p_send.at[r], p_recv.at[r], pair, mp)

    for r in range(2):
        half = 1 - xh if r == 0 else xh
        for side in range(2):
            for t in range(2):
                pair_send[r, side, :, t * 768 : (t + 1) * 768] = product(
                    side, 2 * half + 1 - core, t
                ).astype(BF16)
        pair_copy(r).start()

    @pl.loop(1, NY)
    def _(d):
        block_arrival(d).wait_recv()
        forward(d).start()

    for side in range(2):
        for t in range(2):
            sides[side][2][:, t * 768 : (t + 1) * 768] = product(side, dp, t)

    pair_copy(0).wait_recv()
    for side in range(2):
        for t in range(2):
            cols = slice(t * 768, (t + 1) * 768)
            xh_send[side, :, cols] = (
                product(side, far, t) + pair_recv[0, side, :, cols].astype(F32)
            ).astype(BF16)
    far_copy = remote(xh_send, xh_recv, h_send, h_recv, far, mp)
    far_copy.start()

    own_load.wait()

    @pl.loop(1, NY)
    def _(d):
        gather_arrival(d).wait_recv()
        forward_arrival(d).wait_recv()

    packed = jnp.zeros((TOK, LANE), F32)
    for i in range(NY):
        packed += gpg[:, i * LANE : (i + 1) * LANE].astype(F32)
    tr_s[:TOK, :] = packed
    for b in range(2):
        st_t[:, b * 128 : (b + 1) * 128] = tr_s[b * 128 : (b + 1) * 128, :].T
    xst_send[...] = st_t[HID : HID + 8, :]
    stat_copy = remote(xst_send, xst_recv, s_send, s_recv, dp, xl_mp)
    stat_copy.start()

    def hidden_sum(which):
        cols = pl.ds(pl.multiple_of(which * XCOL, XCOL), XCOL)
        return jnp.dot(gpg[...], wg[:, cols], preferred_element_type=F32)

    xl_send[...] = hidden_sum(1 - xl).astype(BF16)
    half_copy = remote(xl_send, xl_recv, l_send, l_recv, dp, xl_mp)
    half_copy.start()
    gg_s[TOK:, :] = jnp.zeros((256 - TOK, XCOL), F32)
    gg_s[:TOK, :] = hidden_sum(xl)

    half_copy.wait_recv()
    gg_s[:TOK, :] += xl_recv[...].astype(F32)
    for c in range(XCOL // 128):
        for b in range(2):
            gg_t[c * 128 : (c + 1) * 128, b * 128 : (b + 1) * 128] = gg_s[
                b * 128 : (b + 1) * 128, c * 128 : (c + 1) * 128
            ].T
    stat_copy.wait_recv()
    stats = xst_send[...] + xst_recv[...]
    one_hi, one_lo = hi_lo(stats[0:1] + stats[1:2])
    two_hi, two_lo = hi_lo(stats[2:3] + stats[3:4])
    sub = lax.broadcasted_iota(jnp.int32, (8, 256), 0)
    tail8 = jnp.where(sub == 0, one_hi, 0.0)
    tail8 = jnp.where(sub == 1, one_lo, tail8)
    tail8 = jnp.where(sub == 2, two_hi, tail8)
    tail8 = jnp.where(sub == 3, two_lo, tail8)

    def piece_copy(d):
        return remote(z_send.at[d], z_recv.at[d], zs_sem.at[d], zr_sem.at[d], dp, z_mp((z + d) % NZ))

    def piece(place):
        return jnp.concatenate(
            [gg_t[pl.ds(pl.multiple_of(place * PIECE, 8), PIECE), :], tail8], axis=0
        )

    @pl.loop(1, NZ)
    def _(d):
        z_send[d] = piece((z + d) % NZ).astype(BF16)
        piece_copy(d).start()

    last_send[...] = piece(z)

    @pl.loop(1, NZ)
    def _(d):
        piece_copy(d).wait_recv()
        last_send[...] += z_recv[d].astype(F32)

    last_copy = remote(last_send, last_recv, e_send, e_recv, dp, to_mp)

    @pl.when(moves)
    def _():
        last_copy.start()

    @pl.when(to_mp == mp)
    def _():
        last_recv[...] = last_send[...]

    pair_copy(1).wait_recv()
    far_copy.wait_recv()
    for side in range(2):
        out = sides[side][2]
        out[...] += pair_recv[1, side].astype(F32) + xh_recv[side].astype(F32)

    base = pl.multiple_of(jnp.minimum((mp * PIECE) // 128 * 128, D - 256), 128)
    off = mp * PIECE - base
    span = pl.ds(base, 256)
    picks = lax.broadcasted_iota(jnp.int32, (32, 256), 1) == (
        lax.broadcasted_iota(jnp.int32, (32, 256), 0) + off
    )
    pick = jnp.where(picks, 1.0, 0.0)
    x_t = contract_last(pick.astype(BF16), x_v[:, span])[:PIECE]
    go_t = contract_last(pick.astype(BF16), go_v[:, span])[:PIECE]
    gain_t = jnp.sum(pick * gain_ref[:, span], axis=1, keepdims=True)[:PIECE]
    stat_s[TOK:, :] = jnp.zeros((256 - TOK, LANE), F32)
    for b in range(2):
        st_t[:, b * 128 : (b + 1) * 128] = stat_s[b * 128 : (b + 1) * 128, :].T
    mean_row, inv_row = st_t[0:1, :TOK], st_t[64:65, :TOK]
    normed = (x_t - mean_row) * inv_row
    full = last_send[PIECE:, :TOK]
    mean_one = (full[0:1] + full[1:2]) * (1.0 / D)
    mean_two = (full[2:3] + full[3:4]) * (1.0 / D)

    @pl.when(moves)
    def _():
        last_copy.wait_recv()

    grad_normed = last_recv[:PIECE, :TOK] * gain_t
    gi_ref[...] = (go_t + inv_row * (grad_normed - mean_one - normed * mean_two)).astype(BF16)

    @pl.loop(1, NY)
    def _(d):
        block_copy(d).wait_send()
        forward(d).wait_send()
        gather_copy(d).wait_send()

    for r in range(2):
        pair_copy(r).wait_send()
    far_copy.wait_send()
    stat_copy.wait_send()
    half_copy.wait_send()

    @pl.loop(1, NZ)
    def _(d):
        piece_copy(d).wait_send()

    @pl.when(moves)
    def _():
        last_copy.wait_send()


def shards(block_input, grad_out, ln_gain, w_in, w_out):
    dma = pltpu.SemaphoreType.DMA
    grad_input, grad_w_in, grad_w_out = pl.pallas_call(
        kernel,
        out_shape=(
            jax.ShapeDtypeStruct((PIECE, TOK), BF16),
            jax.ShapeDtypeStruct((HID, QUART), F32),
            jax.ShapeDtypeStruct((HID, QUART), F32),
        ),
        in_specs=[
            pl.BlockSpec(memory_space=pl.ANY),
            pl.BlockSpec(memory_space=pl.ANY),
            pl.BlockSpec(memory_space=pltpu.VMEM),
            pl.BlockSpec(memory_space=pl.ANY),
            pl.BlockSpec(memory_space=pl.ANY),
        ],
        out_specs=[pl.BlockSpec(memory_space=pltpu.VMEM)] * 3,
        scratch_shapes=[
            pltpu.VMEM((TOK, D), BF16),
            pltpu.VMEM((TOK, D), BF16),
            pltpu.VMEM((TOK, D), BF16),
            pltpu.VMEM((LANE, D), BF16),
            pltpu.VMEM((LANE, D), BF16),
            pltpu.VMEM((NY * LANE, YCOL), BF16),
            pltpu.VMEM((TOK, NY * LANE), BF16),
            pltpu.VMEM((16, D), BF16),
            pltpu.VMEM((TOK, LANE), F32),
            pltpu.VMEM((TOK, LANE), F32),
            pltpu.VMEM((16, LANE), F32),
            pltpu.VMEM((256, LANE), F32),
            pltpu.VMEM((256, LANE), F32),
            pltpu.VMEM((LANE, 256), BF16),
            pltpu.VMEM((LANE, 256), BF16),
            pltpu.VMEM((2, 2, HID, QUART), BF16),
            pltpu.VMEM((2, 2, HID, QUART), BF16),
            pltpu.VMEM((2, HID, QUART), BF16),
            pltpu.VMEM((2, HID, QUART), BF16),
            pltpu.VMEM((256, XCOL), F32),
            pltpu.VMEM((XCOL, 256), F32),
            pltpu.VMEM((TOK, XCOL), BF16),
            pltpu.VMEM((TOK, XCOL), BF16),
            pltpu.VMEM((LANE, 256), F32),
            pltpu.VMEM((8, 256), F32),
            pltpu.VMEM((8, 256), F32),
            pltpu.VMEM((NZ, 32, 256), BF16),
            pltpu.VMEM((NZ, 32, 256), BF16),
            pltpu.VMEM((32, 256), F32),
            pltpu.VMEM((32, 256), F32),
            dma((4,)), dma((4,)),
            dma((NY,)), dma((NY,)), dma((NY,)), dma((NY,)), dma((NY,)), dma((NY,)),
            dma((2,)), dma((2,)), dma, dma, dma, dma, dma, dma,
            dma((NZ,)), dma((NZ,)), dma, dma,
        ],
        compiler_params=pltpu.CompilerParams(
            collective_id=0, has_side_effects=True, vmem_limit_bytes=60 * 1024 * 1024
        ),
        cost_estimate=pl.CostEstimate(
            flops=2 * 5 * TOK * D * HID, bytes_accessed=9 * 1024 * 1024, transcendentals=TOK * HID
        ),
    )(block_input, grad_out, ln_gain.reshape(1, D), w_in.T, w_out)
    return grad_input.T, grad_w_in.T, grad_w_out


def solution(mesh):
    in_specs = (P("dp", None), P("dp", None), P(), P(None, "mp"), P("mp", None))
    out_specs = (P("dp", "mp"), P("dp", "mp"), P("mp", "dp"))
    return jax.shard_map(shards, mesh=mesh, in_specs=in_specs, out_specs=out_specs, check_vma=False)
```

```python
import jax
import jax.numpy as jnp
from jax import lax
from jax.experimental import pallas as pl
from jax.experimental.pallas import tpu as pltpu
from jax.sharding import PartitionSpec as P

F32 = jnp.float32
BF16 = jnp.bfloat16
D = 6144
TOK = 192
HID = 96
LANE = 128
CCOL = D // 8
TPART = TOK // 4
ZCOL = CCOL // 8
PIECE = D // 256
QUART = D // 4
XROWS = 48


def contract_last(left, right):
    return lax.dot_general(left, right, (((1,), (1,)), ((), ())), preferred_element_type=F32)


def remote(src, dst, send, recv, dp, mp):
    return pltpu.make_async_remote_copy(
        src_ref=src,
        dst_ref=dst,
        send_sem=send,
        recv_sem=recv,
        device_id=(dp, mp),
        device_id_type=pl.DeviceIdType.MESH,
    )


def hi_lo(value):
    high = value.astype(BF16).astype(F32)
    return high, (value - high).astype(BF16).astype(F32)


def in_lanes(rows, first, one, two):
    lanes = lax.broadcasted_iota(jnp.int32, (rows, LANE), 1)
    result = jnp.zeros((rows, LANE), F32)
    for k, part in enumerate(hi_lo(one) + hi_lo(two)):
        result = jnp.where(lanes == first + k, part, result)
    return result


def pair_sums(parts):
    return parts[:, 0:1] + parts[:, 1:2], parts[:, 2:3] + parts[:, 3:4]


def kernel(
    x_hbm, go_hbm, gain_ref, win_hbm, wout_hbm,
    gi_ref, gwin_ref, gwout_ref,
    x_v, go_v, g_v, win_v, wout_v, wg, gpg, gain3, pre_s, ga_s, u_s, stat_s, tr_s, gp_t, act_t,
    pair_send, pair_recv, xh_send, xh_recv, gg_s, b_send, b_recv, c_own, c_send, c_recv,
    last_sum, last_send, final, fin_t, fold, unfold,
    x_sem, load_sem, a_send, a_recv, f_send, f_recv, g_send, g_recv, p_send, p_recv,
    h_send, h_recv, bs_sem, br_sem, cs_sem, cr_sem, e_send, e_recv,
):
    dp = lax.axis_index("dp")
    mp = lax.axis_index("mp")
    xh, core = dp // 2, dp % 2
    z, xl, y = mp // 16, (mp // 8) % 2, mp % 8
    zh, zl, yh, yl = z // 2, z % 2, y // 2, y % 2
    cube = 4 * xl + 2 * yl + zl
    pair = 2 * xh + (1 - core)
    far = 2 * (1 - xh) + core

    def place(in_cube, on_y, on_z):
        zp = 2 * on_z + in_cube % 2
        return zp * 16 + (in_cube // 4) * 8 + 2 * on_y + (in_cube // 2) % 2

    def flip(d):
        return (
            4 * ((xl + d // 4) % 2) + 2 * ((yl + (d // 2) % 2) % 2) + (zl + d % 2) % 2
        )

    def cube_mp(d):
        return place(flip(d), yh, zh)

    def y_mp(d):
        return place(cube, (yh + d) % 4, zh)

    def z_mp(d):
        return place(cube, yh, (zh + d) % 8)

    def owner(k):
        return 32 * cube + 4 * zh + k

    def holder(k):
        return place(mp // 32, k, (mp % 32) // 4)

    own_owner = mp // 4 == 8 * cube + zh

    x_loads = [
        pltpu.make_async_copy(
            x_hbm.at[pl.ds(i * XROWS, XROWS)], x_v.at[pl.ds(i * XROWS, XROWS)], x_sem.at[i]
        )
        for i in range(TOK // XROWS)
    ]
    win_load = pltpu.make_async_copy(win_hbm, win_v.at[pl.ds(0, HID)], load_sem.at[0])
    wout_load = pltpu.make_async_copy(wout_hbm, wout_v.at[pl.ds(0, HID)], load_sem.at[1])
    go_load = pltpu.make_async_copy(go_hbm, go_v, load_sem.at[2])
    own_cols = pl.ds(pl.multiple_of(cube * CCOL, CCOL), CCOL)
    own_load = pltpu.make_async_copy(
        win_hbm.at[:, own_cols],
        wg.at[pl.ds(pl.multiple_of(cube * LANE, LANE), HID)],
        load_sem.at[3],
    )
    for load in x_loads:
        load.start()
    win_load.start()
    wout_load.start()
    go_load.start()
    own_load.start()

    barrier = pltpu.get_barrier_semaphore()

    def greet(to_dp, to_mp_):
        pl.semaphore_signal(
            barrier, inc=1, device_id=(to_dp, to_mp_), device_id_type=pl.DeviceIdType.MESH
        )

    @pl.loop(1, 8)
    def _(d):
        greet(dp, cube_mp(d))
        greet(dp, z_mp(d))

    @pl.loop(1, 4)
    def _(d):
        greet(dp, y_mp(d))

    greet(pair, mp)
    greet(far, mp)
    for k in range(4):

        @pl.when(owner(k) != mp)
        def _():
            greet(dp, owner(k))

        @pl.when(holder(k) != mp)
        def _():
            greet(dp, holder(k))

    pl.semaphore_wait(barrier, 7 + 7 + 3 + 2 + jnp.where(own_owner, 6, 8))

    def block_copy(d):
        return remote(
            win_hbm.at[pl.ds(pl.multiple_of(core * 48, 16), 48), pl.ds(pl.multiple_of(flip(d) * CCOL, CCOL), CCOL)],
            wg.at[pl.ds(pl.multiple_of(cube * LANE + core * 48, 16), 48)],
            a_send.at[d], a_recv.at[d], dp, cube_mp(d),
        )

    def landed(d, half):
        return wg.at[pl.ds(pl.multiple_of(flip(d) * LANE + half * 48, 16), 48)]

    def block_arrival(d):
        return remote(
            landed(d, core), landed(d, core), a_send.at[d], a_recv.at[d], dp, cube_mp(d)
        )

    def forward(d):
        return remote(landed(d, core), landed(d, core), f_send.at[d], f_recv.at[d], pair, mp)

    def forward_arrival(d):
        there = landed(d, 1 - core)
        return remote(there, there, f_send.at[d], f_recv.at[d], pair, mp)

    @pl.loop(1, 8)
    def _(d):
        block_copy(d).start()

    for i in range(8):
        wg[i * LANE + HID : (i + 1) * LANE, :] = jnp.zeros((LANE - HID, CCOL), BF16)
    win_v[HID:, :] = jnp.zeros((LANE - HID, D), BF16)
    wout_v[HID:, :] = jnp.zeros((LANE - HID, D), BF16)

    from_lane = lax.broadcasted_iota(jnp.int32, (LANE, LANE), 0)
    to_lane = lax.broadcasted_iota(jnp.int32, (LANE, LANE), 1)
    for g in range(3):
        in_data = jnp.where(to_lane >= 32 * g, jnp.where(to_lane < 32 * g + PIECE, 1.0, 0.0), 0.0)
        in_tail = jnp.where(
            to_lane >= 32 * g + PIECE, jnp.where(to_lane < 32 * g + PIECE + 4, 1.0, 0.0), 0.0
        )
        tail_hit = jnp.where(from_lane == to_lane + (ZCOL - PIECE - 32 * g), in_tail, 0.0)
        for k in range(4):
            hit = jnp.where(from_lane == to_lane + (PIECE * k - 32 * g), in_data, 0.0) + tail_hit
            fold[g * LANE : (g + 1) * LANE, k * LANE : (k + 1) * LANE] = hit.astype(BF16)
    from_row = lax.broadcasted_iota(jnp.int32, (16, 256), 0)
    token = lax.broadcasted_iota(jnp.int32, (16, 256), 1)
    for g in range(3):
        unfold[g, 64:, :] = jnp.zeros((64, 256), BF16)
        for i in range(4):
            unfold[g, i * 16 : (i + 1) * 16, :] = jnp.where(
                token == from_row + (TPART * i + 16 * g), 1.0, 0.0
            ).astype(BF16)

    lane = lax.broadcasted_iota(jnp.int32, (16, LANE), 1)
    for i in range(TOK // XROWS):
        x_loads[i].wait()

        @pl.loop(0, XROWS // 16)
        def _(t):
            rows = pl.ds(pl.multiple_of(i * XROWS + t * 16, 16), 16)
            tile = x_v[rows, :].astype(F32)
            mean = jnp.sum(tile, axis=1, keepdims=True) * (1.0 / D)
            centred = tile - mean
            inv = lax.rsqrt(jnp.sum(centred * centred, axis=1, keepdims=True) * (1.0 / D) + 1e-06)
            g_v[rows, :] = (centred * inv * gain_ref[...]).astype(BF16)
            stat_s[rows, :] = jnp.where(lane < 64, mean, inv)

    gain = gain_ref[...]
    g_hi = gain.astype(BF16).astype(F32)
    g_mid = (gain - g_hi).astype(BF16).astype(F32)
    g_low = gain - g_hi - g_mid
    row = lax.broadcasted_iota(jnp.int32, (16, D), 0)
    gain3[...] = jnp.where(
        row == 0, g_hi, jnp.where(row == 1, g_mid, jnp.where(row == 2, g_low, 0.0))
    ).astype(BF16)

    win_load.wait()
    wout_load.wait()
    go_load.wait()
    pre_s[...] = jnp.zeros_like(pre_s)
    ga_s[...] = jnp.zeros_like(ga_s)
    u_s[...] = jnp.zeros_like(u_s)

    @pl.loop(0, 4)
    def _(k):
        part = pl.ds(pl.multiple_of(k * 1536, 1536), 1536)
        w_part = win_v[:, part]
        pre_s[...] += contract_last(g_v[:, part], w_part)
        u_s[...] += contract_last(gain3[:, part], w_part)
        ga_s[...] += contract_last(go_v[:, part], wout_v[:, part])

    pre = pre_s[...]
    cdf = 0.5 * (1.0 + lax.erf(pre * 0.7071067811865476))
    act = (pre * cdf).astype(BF16).astype(F32)
    slope = cdf + pre * jnp.exp(-0.5 * pre * pre) * 0.3989422804014327
    gp = (ga_s[...] * slope).astype(BF16).astype(F32)
    u_row = jnp.sum(u_s[...], axis=0, keepdims=True)
    sum_one = jnp.sum(gp * u_row, axis=1, keepdims=True)
    sum_two = jnp.sum(gp * pre, axis=1, keepdims=True)
    own_block = pl.ds(pl.multiple_of(cube * LANE, LANE), LANE)
    gpg[:, own_block] = (gp + in_lanes(TOK, HID, sum_one, sum_two)).astype(BF16)

    def gather_copy(d):
        mine = gpg.at[:, own_block]
        return remote(mine, mine, g_send.at[d], g_recv.at[d], dp, cube_mp(d))

    def gather_arrival(d):
        there = gpg.at[:, pl.ds(pl.multiple_of(flip(d) * LANE, LANE), LANE)]
        return remote(there, there, g_send.at[d], g_recv.at[d], dp, cube_mp(d))

    @pl.loop(1, 8)
    def _(d):
        gather_copy(8 - d).start()

    @pl.loop(1, 8)
    def _(d):
        block_arrival(d).wait_recv()
        forward(d).start()

    tr_s[TOK:, :] = jnp.zeros((256 - TOK, LANE), F32)
    for values, target in ((gp, gp_t), (act, act_t)):
        tr_s[:TOK, :] = values
        for b in range(2):
            target[:, b * 128 : (b + 1) * 128] = tr_s[b * 128 : (b + 1) * 128, :].T.astype(BF16)
    sides = ((gp_t, g_v, gwin_ref), (act_t, go_v, gwout_ref))

    def product(side, quarter, t):
        left, right, _ = sides[side]
        cols = pl.ds(pl.multiple_of(quarter * QUART + t * 768, 128), 768)
        return jnp.dot(left[:HID, :TOK], right[:, cols], preferred_element_type=F32)

    def pair_copy(r):
        return remote(pair_send.at[r], pair_recv.at[r], p_send.at[r], p_recv.at[r], pair, mp)

    for r in range(2):
        half = 1 - xh if r == 0 else xh
        for side in range(2):
            for t in range(2):
                pair_send[r, side, :, t * 768 : (t + 1) * 768] = product(
                    side, 2 * half + 1 - core, t
                ).astype(BF16)
        pair_copy(r).start()

    for side in range(2):
        for t in range(2):
            sides[side][2][:, t * 768 : (t + 1) * 768] = product(side, dp, t)

    pair_copy(0).wait_recv()
    for side in range(2):
        for t in range(2):
            cols = slice(t * 768, (t + 1) * 768)
            xh_send[side, :, cols] = (
                product(side, far, t) + pair_recv[0, side, :, cols].astype(F32)
            ).astype(BF16)
    far_copy = remote(xh_send, xh_recv, h_send, h_recv, far, mp)
    far_copy.start()

    own_load.wait()

    @pl.loop(1, 8)
    def _(d):
        gather_arrival(d).wait_recv()
        forward_arrival(d).wait_recv()

    packed = jnp.zeros((TOK, LANE), F32)
    for i in range(8):
        packed += gpg[:, i * LANE : (i + 1) * LANE].astype(F32)
    gg_s[:, CCOL:] = in_lanes(TOK, 0, *pair_sums(packed[:, HID : HID + 4]))
    gg_s[:, :CCOL] = jnp.dot(gpg[...], wg[...], preferred_element_type=F32)

    def token_rows(d):
        return pl.ds(pl.multiple_of((yh + d) % 4 * TPART, 16), TPART)

    def token_copy(d):
        return remote(b_send.at[d], b_recv.at[d], bs_sem.at[d], br_sem.at[d], dp, y_mp(d))

    for d in (2, 1, 3):
        b_send[d] = gg_s[token_rows(d), :].astype(BF16)
        token_copy(d).start()

    part = gg_s[token_rows(0), :]
    for d in range(1, 4):
        token_copy(d).wait_recv()
        part += b_recv[d].astype(F32)

    lanes = lax.broadcasted_iota(jnp.int32, (TPART, LANE), 1)
    tail = in_lanes(TPART, ZCOL, *pair_sums(part[:, CCOL : CCOL + 4]))
    for k in range(8):
        piece = jnp.where(lanes < ZCOL, part[:, k * ZCOL : k * ZCOL + LANE], tail)
        c_own[k] = piece
        c_send[k] = piece.astype(BF16)

    def column_copy(d):
        return remote(
            c_send.at[(zh + d) % 8], c_recv.at[d], cs_sem.at[d], cr_sem.at[d], dp, z_mp(d)
        )

    far_first = (4, 3, 5, 2, 6, 1, 7)
    for d in far_first:
        column_copy(d).start()

    last_sum[...] = c_own[zh]
    for d in far_first:
        column_copy(d).wait_recv()
        last_sum[...] += c_recv[d].astype(F32)

    summed = last_sum[...]
    tail = in_lanes(TPART, ZCOL, *pair_sums(summed[:, ZCOL : ZCOL + 4]))
    rounded = jnp.where(lanes < ZCOL, summed, tail).astype(BF16)
    folded = jnp.dot(
        jnp.concatenate([rounded[16 * g : 16 * (g + 1)] for g in range(3)], axis=1),
        fold[...],
        preferred_element_type=F32,
    ).astype(BF16)
    for k in range(4):
        last_send[k] = folded[:, k * LANE : (k + 1) * LANE]

    def last_copy(k):
        return remote(
            last_send.at[k], final.at[yh], e_send.at[k], e_recv.at[yh], dp, owner(k)
        )

    def last_arrival(k):
        return remote(final.at[k], final.at[k], e_send.at[k], e_recv.at[k], dp, holder(k))

    for k in range(4):

        @pl.when(owner(k) != mp)
        def _():
            last_copy(k).start()

    @pl.when(own_owner)
    def _():
        final[yh] = last_send[mp % 4]

    pair_copy(1).wait_recv()
    far_copy.wait_recv()
    for side in range(2):
        out = sides[side][2]
        out[...] += pair_recv[1, side].astype(F32) + xh_recv[side].astype(F32)

    base = pl.multiple_of(jnp.minimum((mp * PIECE) // 128 * 128, D - 256), 128)
    off = mp * PIECE - base
    span = pl.ds(base, 256)
    picks = lax.broadcasted_iota(jnp.int32, (32, 256), 1) == (
        lax.broadcasted_iota(jnp.int32, (32, 256), 0) + off
    )
    pick = jnp.where(picks, 1.0, 0.0)
    x_t = contract_last(pick.astype(BF16), x_v[:, span])[:PIECE]
    go_t = contract_last(pick.astype(BF16), go_v[:, span])[:PIECE]
    gain_t = jnp.sum(pick * gain_ref[:, span], axis=1, keepdims=True)[:PIECE]
    stat_s[TOK:, :] = jnp.zeros((256 - TOK, LANE), F32)
    for b in range(2):
        fin_t[:, b * 128 : (b + 1) * 128] = stat_s[b * 128 : (b + 1) * 128, :].T
    mean_row, inv_row = fin_t[0:1, :TOK], fin_t[64:65, :TOK]
    normed = (x_t - mean_row) * inv_row

    for k in range(4):

        @pl.when(holder(k) != mp)
        def _():
            last_arrival(k).wait_recv()

    tr_s[64:128, :] = jnp.zeros((64, LANE), F32)
    for i in range(4):
        tr_s[i * 16 : (i + 1) * 16, :] = final[i].astype(F32)
    turned = tr_s[:128, :].T.astype(BF16)
    laid = jnp.zeros((32, 256), F32)
    for g in range(3):
        laid += jnp.dot(turned[32 * g : 32 * (g + 1)], unfold[g], preferred_element_type=F32)
    laid = laid[:, :TOK]
    grad_normed = laid[:PIECE] * gain_t
    mean_one = (laid[PIECE : PIECE + 1] + laid[PIECE + 1 : PIECE + 2]) * (1.0 / D)
    mean_two = (laid[PIECE + 2 : PIECE + 3] + laid[PIECE + 3 : PIECE + 4]) * (1.0 / D)
    gi_ref[...] = (go_t + inv_row * (grad_normed - mean_one - normed * mean_two)).astype(BF16)

    @pl.loop(1, 8)
    def _(d):
        block_copy(d).wait_send()
        forward(d).wait_send()
        gather_copy(d).wait_send()
        column_copy(d).wait_send()

    for r in range(2):
        pair_copy(r).wait_send()
    far_copy.wait_send()

    @pl.loop(1, 4)
    def _(d):
        token_copy(d).wait_send()

    for k in range(4):

        @pl.when(owner(k) != mp)
        def _():
            last_copy(k).wait_send()


def place_outputs(gi, gwin, gwout, gi_out, gwin_out, gwout_out, gi_v, w_v, in_sem, out_sem):
    parts = [(gi, gi_v, gi_out)]
    for side, (array, out) in enumerate(((gwin, gwin_out), (gwout, gwout_out))):
        for k in range(4):
            rows = pl.ds(k * 24, 24)
            parts.append((array.at[rows], w_v.at[side, rows], out.at[rows]))
    reads, writes = [], []
    for k, (array, held, out) in enumerate(parts):
        reads.append(pltpu.make_async_copy(array, held, in_sem.at[k]))
        writes.append(pltpu.make_async_copy(held, out, out_sem.at[k]))
    for read in reads:
        read.start()
    for read, write in zip(reads, writes):
        read.wait()
        write.start()
    for write in writes:
        write.wait()


def shards(block_input, grad_out, ln_gain, w_in, w_out):
    dma = pltpu.SemaphoreType.DMA
    grad_input, grad_w_in, grad_w_out = pl.pallas_call(
        kernel,
        out_shape=(
            jax.ShapeDtypeStruct((PIECE, TOK), BF16),
            jax.ShapeDtypeStruct((HID, QUART), F32),
            jax.ShapeDtypeStruct((HID, QUART), F32),
        ),
        in_specs=[
            pl.BlockSpec(memory_space=pl.ANY),
            pl.BlockSpec(memory_space=pl.ANY),
            pl.BlockSpec(memory_space=pltpu.VMEM),
            pl.BlockSpec(memory_space=pl.ANY),
            pl.BlockSpec(memory_space=pl.ANY),
        ],
        out_specs=[pl.BlockSpec(memory_space=pltpu.VMEM)] * 3,
        scratch_shapes=[
            pltpu.VMEM((TOK, D), BF16),
            pltpu.VMEM((TOK, D), BF16),
            pltpu.VMEM((TOK, D), BF16),
            pltpu.VMEM((LANE, D), BF16),
            pltpu.VMEM((LANE, D), BF16),
            pltpu.VMEM((8 * LANE, CCOL), BF16),
            pltpu.VMEM((TOK, 8 * LANE), BF16),
            pltpu.VMEM((16, D), BF16),
            pltpu.VMEM((TOK, LANE), F32),
            pltpu.VMEM((TOK, LANE), F32),
            pltpu.VMEM((16, LANE), F32),
            pltpu.VMEM((256, LANE), F32),
            pltpu.VMEM((256, LANE), F32),
            pltpu.VMEM((LANE, 256), BF16),
            pltpu.VMEM((LANE, 256), BF16),
            pltpu.VMEM((2, 2, HID, QUART), BF16),
            pltpu.VMEM((2, 2, HID, QUART), BF16),
            pltpu.VMEM((2, HID, QUART), BF16),
            pltpu.VMEM((2, HID, QUART), BF16),
            pltpu.VMEM((TOK, CCOL + LANE), F32),
            pltpu.VMEM((4, TPART, CCOL + LANE), BF16),
            pltpu.VMEM((4, TPART, CCOL + LANE), BF16),
            pltpu.VMEM((8, TPART, LANE), F32),
            pltpu.VMEM((8, TPART, LANE), BF16),
            pltpu.VMEM((8, TPART, LANE), BF16),
            pltpu.VMEM((TPART, LANE), F32),
            pltpu.VMEM((4, 16, LANE), BF16),
            pltpu.VMEM((4, 16, LANE), BF16),
            pltpu.VMEM((LANE, 256), F32),
            pltpu.VMEM((3 * LANE, 4 * LANE), BF16),
            pltpu.VMEM((3, LANE, 256), BF16),
            dma((4,)), dma((4,)),
            dma((8,)), dma((8,)), dma((8,)), dma((8,)), dma((8,)), dma((8,)),
            dma((2,)), dma((2,)), dma, dma,
            dma((4,)), dma((4,)), dma((8,)), dma((8,)), dma((4,)), dma((4,)),
        ],
        compiler_params=pltpu.CompilerParams(
            collective_id=0, has_side_effects=True, vmem_limit_bytes=60 * 1024 * 1024
        ),
        cost_estimate=pl.CostEstimate(
            flops=2 * 5 * TOK * D * HID, bytes_accessed=9 * 1024 * 1024, transcendentals=TOK * HID
        ),
    )(block_input, grad_out, ln_gain.reshape(1, D), w_in.T, w_out)
    grad_input, grad_w_in, grad_w_out = pl.pallas_call(
        place_outputs,
        out_shape=(
            jax.ShapeDtypeStruct((PIECE, TOK), BF16),
            jax.ShapeDtypeStruct((HID, QUART), F32),
            jax.ShapeDtypeStruct((HID, QUART), F32),
        ),
        in_specs=[pl.BlockSpec(memory_space=pl.ANY)] * 3,
        out_specs=[pl.BlockSpec(memory_space=pl.ANY)] * 3,
        scratch_shapes=[
            pltpu.VMEM((PIECE, TOK), BF16),
            pltpu.VMEM((2, HID, QUART), F32),
            dma((9,)),
            dma((9,)),
        ],
        compiler_params=pltpu.CompilerParams(vmem_limit_bytes=60 * 1024 * 1024),
    )(grad_input, grad_w_in, grad_w_out)
    return grad_input.T, grad_w_in.T, grad_w_out


def solution(mesh):
    in_specs = (P("dp", None), P("dp", None), P(), P(None, "mp"), P("mp", None))
    out_specs = (P("dp", "mp"), P("dp", "mp"), P("mp", "dp"))
    return jax.shard_map(shards, mesh=mesh, in_specs=in_specs, out_specs=out_specs, check_vma=False)
```

```python
import jax
import jax.numpy as jnp
from jax import lax
from jax.experimental import pallas as pl
from jax.experimental.pallas import tpu as pltpu
from jax.sharding import PartitionSpec as P

F32 = jnp.float32
BF16 = jnp.bfloat16
D = 6144
TOK = 192
HID = 96
LANE = 128
CCOL = D // 8
TPART = TOK // 4
ZCOL = CCOL // 8
PIECE = D // 256
QUART = D // 4
XROWS = 48


def contract_last(left, right):
    return lax.dot_general(left, right, (((1,), (1,)), ((), ())), preferred_element_type=F32)


def remote(src, dst, send, recv, dp, mp):
    return pltpu.make_async_remote_copy(
        src_ref=src,
        dst_ref=dst,
        send_sem=send,
        recv_sem=recv,
        device_id=(dp, mp),
        device_id_type=pl.DeviceIdType.MESH,
    )


def hi_lo(value):
    high = value.astype(BF16).astype(F32)
    return high, (value - high).astype(BF16).astype(F32)


def in_lanes(rows, first, one, two):
    lanes = lax.broadcasted_iota(jnp.int32, (rows, LANE), 1)
    result = jnp.zeros((rows, LANE), F32)
    for k, part in enumerate(hi_lo(one) + hi_lo(two)):
        result = jnp.where(lanes == first + k, part, result)
    return result


def pair_sums(parts):
    return parts[:, 0:1] + parts[:, 1:2], parts[:, 2:3] + parts[:, 3:4]


def kernel(
    x_hbm, go_hbm, gain_ref, win_hbm, wout_hbm,
    gi_ref, gwin_ref, gwout_ref,
    x_v, go_v, g_v, win_v, wout_v, wg, gpg, gain3, pre_s, ga_s, u_s, stat_s, tr_s, gp_t, act_t,
    pair_send, pair_recv, xh_send, xh_recv, gg_s, b_send, b_recv, c_own, c_send, c_recv,
    o_own, o_send, o_recv, t_own, t_send, t_recv, last_send, final, fin_t, fold, unfold,
    x_sem, load_sem, a_send, a_recv, f_send, f_recv, g_send, g_recv, p_send, p_recv,
    h_send, h_recv, bs_sem, br_sem, cs_sem, cr_sem, os_sem, or_sem, ts_sem, tr_sem, e_send, e_recv,
):
    dp = lax.axis_index("dp")
    mp = lax.axis_index("mp")
    xh, core = dp // 2, dp % 2
    z, xl, y = mp // 16, (mp // 8) % 2, mp % 8
    zh, zl, yh, yl = z // 2, z % 2, y // 2, y % 2
    cube = 4 * xl + 2 * yl + zl
    pair = 2 * xh + (1 - core)
    far = 2 * (1 - xh) + core

    def place(in_cube, on_y, on_z):
        zp = 2 * on_z + in_cube % 2
        return zp * 16 + (in_cube // 4) * 8 + 2 * on_y + (in_cube // 2) % 2

    def flip(d):
        return (
            4 * ((xl + d // 4) % 2) + 2 * ((yl + (d // 2) % 2) % 2) + (zl + d % 2) % 2
        )

    def cube_mp(d):
        return place(flip(d), yh, zh)

    def y_mp(d):
        return place(cube, (yh + d) % 4, zh)

    def z_mp(d):
        return place(cube, yh, (zh + d) % 8)

    def owner(k):
        return 32 * cube + 4 * zh + k

    def holder(k):
        return place(mp // 32, k, (mp % 32) // 4)

    own_owner = mp // 4 == 8 * cube + zh

    x_loads = [
        pltpu.make_async_copy(
            x_hbm.at[pl.ds(i * XROWS, XROWS)], x_v.at[pl.ds(i * XROWS, XROWS)], x_sem.at[i]
        )
        for i in range(TOK // XROWS)
    ]
    win_load = pltpu.make_async_copy(win_hbm, win_v.at[pl.ds(0, HID)], load_sem.at[0])
    wout_load = pltpu.make_async_copy(wout_hbm, wout_v.at[pl.ds(0, HID)], load_sem.at[1])
    go_load = pltpu.make_async_copy(go_hbm, go_v, load_sem.at[2])
    own_cols = pl.ds(pl.multiple_of(cube * CCOL, CCOL), CCOL)
    own_load = pltpu.make_async_copy(
        win_hbm.at[:, own_cols],
        wg.at[pl.ds(pl.multiple_of(cube * LANE, LANE), HID)],
        load_sem.at[3],
    )
    for load in x_loads:
        load.start()
    win_load.start()
    wout_load.start()
    go_load.start()
    own_load.start()

    barrier = pltpu.get_barrier_semaphore()

    def greet(to_dp, to_mp_):
        pl.semaphore_signal(
            barrier, inc=1, device_id=(to_dp, to_mp_), device_id_type=pl.DeviceIdType.MESH
        )

    @pl.loop(1, 8)
    def _(d):
        greet(dp, cube_mp(d))
        greet(dp, z_mp(d))

    @pl.loop(1, 4)
    def _(d):
        greet(dp, y_mp(d))

    greet(pair, mp)
    greet(far, mp)
    for k in range(4):

        @pl.when(owner(k) != mp)
        def _():
            greet(dp, owner(k))

        @pl.when(holder(k) != mp)
        def _():
            greet(dp, holder(k))

    pl.semaphore_wait(barrier, 7 + 7 + 3 + 2 + jnp.where(own_owner, 6, 8))

    def block_copy(d):
        return remote(
            win_hbm.at[pl.ds(pl.multiple_of(core * 48, 16), 48), pl.ds(pl.multiple_of(flip(d) * CCOL, CCOL), CCOL)],
            wg.at[pl.ds(pl.multiple_of(cube * LANE + core * 48, 16), 48)],
            a_send.at[d], a_recv.at[d], dp, cube_mp(d),
        )

    def landed(d, half):
        return wg.at[pl.ds(pl.multiple_of(flip(d) * LANE + half * 48, 16), 48)]

    def block_arrival(d):
        return remote(
            landed(d, core), landed(d, core), a_send.at[d], a_recv.at[d], dp, cube_mp(d)
        )

    def forward(d):
        return remote(landed(d, core), landed(d, core), f_send.at[d], f_recv.at[d], pair, mp)

    def forward_arrival(d):
        there = landed(d, 1 - core)
        return remote(there, there, f_send.at[d], f_recv.at[d], pair, mp)

    @pl.loop(1, 8)
    def _(d):
        block_copy(d).start()

    win_v[HID:, :] = jnp.zeros((LANE - HID, D), BF16)
    wout_v[HID:, :] = jnp.zeros((LANE - HID, D), BF16)

    gain = gain_ref[...]
    g_hi = gain.astype(BF16).astype(F32)
    g_mid = (gain - g_hi).astype(BF16).astype(F32)
    g_low = gain - g_hi - g_mid
    row = lax.broadcasted_iota(jnp.int32, (16, D), 0)
    gain3[...] = jnp.where(
        row == 0, g_hi, jnp.where(row == 1, g_mid, jnp.where(row == 2, g_low, 0.0))
    ).astype(BF16)

    lane = lax.broadcasted_iota(jnp.int32, (16, LANE), 1)

    def norm_chunk(i):
        x_loads[i].wait()

        @pl.loop(0, XROWS // 16)
        def _(t):
            rows = pl.ds(pl.multiple_of(i * XROWS + t * 16, 16), 16)
            tile = x_v[rows, :].astype(F32)
            mean = jnp.sum(tile, axis=1, keepdims=True) * (1.0 / D)
            centred = tile - mean
            inv = lax.rsqrt(jnp.sum(centred * centred, axis=1, keepdims=True) * (1.0 / D) + 1e-06)
            g_v[rows, :] = (centred * inv * gain_ref[...]).astype(BF16)
            stat_s[rows, :] = jnp.where(lane < 64, mean, inv)

    norm_chunk(0)

    for i in range(1, TOK // XROWS):
        norm_chunk(i)

    win_load.wait()
    wout_load.wait()
    go_load.wait()
    pre_s[...] = jnp.zeros_like(pre_s)
    u_s[...] = jnp.zeros_like(u_s)
    ga_s[...] = jnp.zeros_like(ga_s)

    @pl.loop(0, 4)
    def _(k):
        part = pl.ds(pl.multiple_of(k * 1536, 1536), 1536)
        w_part = win_v[:, part]
        pre_s[...] += contract_last(g_v[:, part], w_part)
        u_s[...] += contract_last(gain3[:, part], w_part)
        ga_s[...] += contract_last(go_v[:, part], wout_v[:, part])

    pre = pre_s[...]
    cdf = 0.5 * (1.0 + lax.erf(pre * 0.7071067811865476))
    act = (pre * cdf).astype(BF16).astype(F32)
    slope = cdf + pre * jnp.exp(-0.5 * pre * pre) * 0.3989422804014327
    gp = (ga_s[...] * slope).astype(BF16).astype(F32)
    u_row = jnp.sum(u_s[...], axis=0, keepdims=True)
    sum_one = jnp.sum(gp * u_row, axis=1, keepdims=True)
    sum_two = jnp.sum(gp * pre, axis=1, keepdims=True)
    own_block = pl.ds(pl.multiple_of(cube * LANE, LANE), LANE)
    gpg[:, own_block] = (gp + in_lanes(TOK, HID, sum_one, sum_two)).astype(BF16)

    def gather_copy(d):
        mine = gpg.at[:, own_block]
        return remote(mine, mine, g_send.at[d], g_recv.at[d], dp, cube_mp(d))

    def gather_arrival(d):
        there = gpg.at[:, pl.ds(pl.multiple_of(flip(d) * LANE, LANE), LANE)]
        return remote(there, there, g_send.at[d], g_recv.at[d], dp, cube_mp(d))

    @pl.loop(1, 8)
    def _(d):
        gather_copy(8 - d).start()

    @pl.loop(1, 8)
    def _(d):
        block_arrival(d).wait_recv()
        forward(d).start()

    for i in range(8):
        wg[i * LANE + HID : (i + 1) * LANE, :] = jnp.zeros((LANE - HID, CCOL), BF16)

    tr_s[TOK:, :] = jnp.zeros((256 - TOK, LANE), F32)
    for values, target in ((gp, gp_t), (act, act_t)):
        tr_s[:TOK, :] = values
        for b in range(2):
            target[:, b * 128 : (b + 1) * 128] = tr_s[b * 128 : (b + 1) * 128, :].T.astype(BF16)
    sides = ((gp_t, g_v, gwin_ref), (act_t, go_v, gwout_ref))

    def product(side, quarter, t):
        left, right, _ = sides[side]
        cols = pl.ds(pl.multiple_of(quarter * QUART + t * 768, 128), 768)
        return jnp.dot(left[:HID, :TOK], right[:, cols], preferred_element_type=F32)

    def pair_copy(r):
        return remote(pair_send.at[r], pair_recv.at[r], p_send.at[r], p_recv.at[r], pair, mp)

    for r in range(2):
        half = 1 - xh if r == 0 else xh
        for side in range(2):
            for t in range(2):
                pair_send[r, side, :, t * 768 : (t + 1) * 768] = product(
                    side, 2 * half + 1 - core, t
                ).astype(BF16)
        pair_copy(r).start()

    for side in range(2):
        for t in range(2):
            sides[side][2][:, t * 768 : (t + 1) * 768] = product(side, dp, t)

    pair_copy(0).wait_recv()
    for side in range(2):
        for t in range(2):
            cols = slice(t * 768, (t + 1) * 768)
            xh_send[side, :, cols] = (
                product(side, far, t) + pair_recv[0, side, :, cols].astype(F32)
            ).astype(BF16)
    far_copy = remote(xh_send, xh_recv, h_send, h_recv, far, mp)
    far_copy.start()

    own_load.wait()

    @pl.loop(1, 8)
    def _(d):
        gather_arrival(d).wait_recv()
        forward_arrival(d).wait_recv()

    packed = jnp.zeros((TOK, LANE), F32)
    for i in range(8):
        packed += gpg[:, i * LANE : (i + 1) * LANE].astype(F32)
    gg_s[:, CCOL:] = in_lanes(TOK, 0, *pair_sums(packed[:, HID : HID + 4]))
    gg_s[:, :CCOL] = jnp.dot(gpg[...], wg[...], preferred_element_type=F32)

    far_first = (4, 3, 5, 2, 6, 1, 7)

    def pieces(values, own, send):
        rows = values.shape[0]
        lanes = lax.broadcasted_iota(jnp.int32, (rows, LANE), 1)
        tail = in_lanes(rows, ZCOL, *pair_sums(values[:, CCOL : CCOL + 4]))
        for k in range(8):
            piece = jnp.where(lanes < ZCOL, values[:, k * ZCOL : k * ZCOL + LANE], tail)
            own[k] = piece
            send[k] = piece.astype(BF16)

    def token_rows(d):
        return pl.ds(pl.multiple_of((yh + d) % 4 * 32, 32), 32)

    def token_copy(d):
        return remote(b_send.at[d], b_recv.at[d], bs_sem.at[d], br_sem.at[d], dp, y_mp(d))

    def column_copy(d):
        return remote(
            c_send.at[(zh + d) % 8], c_recv.at[d], cs_sem.at[d], cr_sem.at[d], dp, z_mp(d)
        )

    def other_column_copy(d):
        return remote(
            o_send.at[(zh + d) % 8], o_recv.at[d], os_sem.at[d], or_sem.at[d], dp, z_mp(d)
        )

    def other_token_copy(d):
        return remote(
            t_send.at[(yh + d) % 4], t_recv.at[d], ts_sem.at[d], tr_sem.at[d], dp, y_mp(d)
        )

    for d in (2, 1, 3):
        b_send[d] = gg_s[token_rows(d), :].astype(BF16)
        token_copy(d).start()
    pieces(gg_s[128:, :], o_own, o_send)
    for d in far_first:
        other_column_copy(d).start()

    from_lane = lax.broadcasted_iota(jnp.int32, (LANE, LANE), 0)
    to_lane = lax.broadcasted_iota(jnp.int32, (LANE, LANE), 1)
    for g in range(3):
        in_data = jnp.where(to_lane >= 32 * g, jnp.where(to_lane < 32 * g + PIECE, 1.0, 0.0), 0.0)
        in_tail = jnp.where(
            to_lane >= 32 * g + PIECE, jnp.where(to_lane < 32 * g + PIECE + 4, 1.0, 0.0), 0.0
        )
        tail_hit = jnp.where(from_lane == to_lane + (ZCOL - PIECE - 32 * g), in_tail, 0.0)
        for k in range(4):
            hit = jnp.where(from_lane == to_lane + (PIECE * k - 32 * g), in_data, 0.0) + tail_hit
            fold[g * LANE : (g + 1) * LANE, k * LANE : (k + 1) * LANE] = hit.astype(BF16)
    from_row = lax.broadcasted_iota(jnp.int32, (16, 256), 0)
    token = lax.broadcasted_iota(jnp.int32, (16, 256), 1)
    for g in range(3):
        unfold[g, 64:, :] = jnp.zeros((64, 256), BF16)
        for i in range(4):
            unfold[g, i * 16 : (i + 1) * 16, :] = jnp.where(
                token == from_row + (32 * i + 16 * g if g < 2 else 128 + 16 * i), 1.0, 0.0
            ).astype(BF16)

    part = gg_s[token_rows(0), :]
    for d in (1, 3, 2):
        token_copy(d).wait_recv()
        part += b_recv[d].astype(F32)
    pieces(part, c_own, c_send)
    for d in far_first:
        column_copy(d).start()

    o_sum = o_own[zh]
    for d in (1, 7, 2, 6, 3, 5, 4):
        other_column_copy(d).wait_recv()
        o_sum += o_recv[d].astype(F32)
    lanes = lax.broadcasted_iota(jnp.int32, (64, LANE), 1)
    tail = in_lanes(64, ZCOL, *pair_sums(o_sum[:, ZCOL : ZCOL + 4]))
    o_sum = jnp.where(lanes < ZCOL, o_sum, tail)
    for k in range(4):
        t_own[k] = o_sum[16 * k : 16 * (k + 1)]
        t_send[k] = t_own[k].astype(BF16)
    for d in (2, 1, 3):
        other_token_copy(d).start()

    c_sum = c_own[zh]
    for d in (1, 7, 2, 6, 3, 5, 4):
        column_copy(d).wait_recv()
        c_sum += c_recv[d].astype(F32)
    t_sum = t_own[yh]
    for d in (1, 3, 2):
        other_token_copy(d).wait_recv()
        t_sum += t_recv[d].astype(F32)

    lanes = lax.broadcasted_iota(jnp.int32, (TPART, LANE), 1)
    summed = jnp.concatenate([c_sum, t_sum], axis=0)
    tail = in_lanes(TPART, ZCOL, *pair_sums(summed[:, ZCOL : ZCOL + 4]))
    rounded = jnp.where(lanes < ZCOL, summed, tail).astype(BF16)
    folded = jnp.dot(
        jnp.concatenate([rounded[16 * g : 16 * (g + 1)] for g in range(3)], axis=1),
        fold[...],
        preferred_element_type=F32,
    ).astype(BF16)
    for k in range(4):
        last_send[k] = folded[:, k * LANE : (k + 1) * LANE]

    def last_copy(k):
        return remote(
            last_send.at[k], final.at[yh], e_send.at[k], e_recv.at[yh], dp, owner(k)
        )

    def last_arrival(k):
        return remote(final.at[k], final.at[k], e_send.at[k], e_recv.at[k], dp, holder(k))

    for k in range(4):

        @pl.when(owner(k) != mp)
        def _():
            last_copy(k).start()

    @pl.when(own_owner)
    def _():
        final[yh] = last_send[mp % 4]

    pair_copy(1).wait_recv()
    far_copy.wait_recv()
    for side in range(2):
        out = sides[side][2]
        out[...] += pair_recv[1, side].astype(F32) + xh_recv[side].astype(F32)

    base = pl.multiple_of(jnp.minimum((mp * PIECE) // 128 * 128, D - 256), 128)
    off = mp * PIECE - base
    span = pl.ds(base, 256)
    picks = lax.broadcasted_iota(jnp.int32, (32, 256), 1) == (
        lax.broadcasted_iota(jnp.int32, (32, 256), 0) + off
    )
    pick = jnp.where(picks, 1.0, 0.0)
    x_t = contract_last(pick.astype(BF16), x_v[:, span])[:PIECE]
    go_t = contract_last(pick.astype(BF16), go_v[:, span])[:PIECE]
    gain_t = jnp.sum(pick * gain_ref[:, span], axis=1, keepdims=True)[:PIECE]
    stat_s[TOK:, :] = jnp.zeros((256 - TOK, LANE), F32)
    for b in range(2):
        fin_t[:, b * 128 : (b + 1) * 128] = stat_s[b * 128 : (b + 1) * 128, :].T
    mean_row, inv_row = fin_t[0:1, :TOK], fin_t[64:65, :TOK]
    normed = (x_t - mean_row) * inv_row

    for k in range(4):

        @pl.when(holder(k) != mp)
        def _():
            last_arrival(k).wait_recv()

    tr_s[64:128, :] = jnp.zeros((64, LANE), F32)
    for i in range(4):
        tr_s[i * 16 : (i + 1) * 16, :] = final[i].astype(F32)
    turned = tr_s[:128, :].T.astype(BF16)
    laid = jnp.zeros((32, 256), F32)
    for g in range(3):
        laid += jnp.dot(turned[32 * g : 32 * (g + 1)], unfold[g], preferred_element_type=F32)
    laid = laid[:, :TOK]
    grad_normed = laid[:PIECE] * gain_t
    mean_one = (laid[PIECE : PIECE + 1] + laid[PIECE + 1 : PIECE + 2]) * (1.0 / D)
    mean_two = (laid[PIECE + 2 : PIECE + 3] + laid[PIECE + 3 : PIECE + 4]) * (1.0 / D)
    gi_ref[...] = (go_t + inv_row * (grad_normed - mean_one - normed * mean_two)).astype(BF16)

    @pl.loop(1, 8)
    def _(d):
        block_copy(d).wait_send()
        forward(d).wait_send()
        gather_copy(d).wait_send()
        column_copy(d).wait_send()
        other_column_copy(d).wait_send()

    for r in range(2):
        pair_copy(r).wait_send()
    far_copy.wait_send()

    @pl.loop(1, 4)
    def _(d):
        token_copy(d).wait_send()
        other_token_copy(d).wait_send()

    for k in range(4):

        @pl.when(owner(k) != mp)
        def _():
            last_copy(k).wait_send()


def place_outputs(gi, gwin, gwout, gi_out, gwin_out, gwout_out, gi_v, w_v, in_sem, out_sem):
    parts = [(gi, gi_v, gi_out)]
    for side, (array, out) in enumerate(((gwin, gwin_out), (gwout, gwout_out))):
        for k in range(4):
            rows = pl.ds(k * 24, 24)
            parts.append((array.at[rows], w_v.at[side, rows], out.at[rows]))
    reads, writes = [], []
    for k, (array, held, out) in enumerate(parts):
        reads.append(pltpu.make_async_copy(array, held, in_sem.at[k]))
        writes.append(pltpu.make_async_copy(held, out, out_sem.at[k]))
    for read in reads:
        read.start()
    for read, write in zip(reads, writes):
        read.wait()
        write.start()
    for write in writes:
        write.wait()


def shards(block_input, grad_out, ln_gain, w_in, w_out):
    dma = pltpu.SemaphoreType.DMA
    grad_input, grad_w_in, grad_w_out = pl.pallas_call(
        kernel,
        out_shape=(
            jax.ShapeDtypeStruct((PIECE, TOK), BF16),
            jax.ShapeDtypeStruct((HID, QUART), F32),
            jax.ShapeDtypeStruct((HID, QUART), F32),
        ),
        in_specs=[
            pl.BlockSpec(memory_space=pl.ANY),
            pl.BlockSpec(memory_space=pl.ANY),
            pl.BlockSpec(memory_space=pltpu.VMEM),
            pl.BlockSpec(memory_space=pl.ANY),
            pl.BlockSpec(memory_space=pl.ANY),
        ],
        out_specs=[pl.BlockSpec(memory_space=pltpu.VMEM)] * 3,
        scratch_shapes=[
            pltpu.VMEM((TOK, D), BF16),
            pltpu.VMEM((TOK, D), BF16),
            pltpu.VMEM((TOK, D), BF16),
            pltpu.VMEM((LANE, D), BF16),
            pltpu.VMEM((LANE, D), BF16),
            pltpu.VMEM((8 * LANE, CCOL), BF16),
            pltpu.VMEM((TOK, 8 * LANE), BF16),
            pltpu.VMEM((16, D), BF16),
            pltpu.VMEM((TOK, LANE), F32),
            pltpu.VMEM((TOK, LANE), F32),
            pltpu.VMEM((16, LANE), F32),
            pltpu.VMEM((256, LANE), F32),
            pltpu.VMEM((256, LANE), F32),
            pltpu.VMEM((LANE, 256), BF16),
            pltpu.VMEM((LANE, 256), BF16),
            pltpu.VMEM((2, 2, HID, QUART), BF16),
            pltpu.VMEM((2, 2, HID, QUART), BF16),
            pltpu.VMEM((2, HID, QUART), BF16),
            pltpu.VMEM((2, HID, QUART), BF16),
            pltpu.VMEM((TOK, CCOL + LANE), F32),
            pltpu.VMEM((4, 32, CCOL + LANE), BF16),
            pltpu.VMEM((4, 32, CCOL + LANE), BF16),
            pltpu.VMEM((8, 32, LANE), F32),
            pltpu.VMEM((8, 32, LANE), BF16),
            pltpu.VMEM((8, 32, LANE), BF16),
            pltpu.VMEM((8, 64, LANE), F32),
            pltpu.VMEM((8, 64, LANE), BF16),
            pltpu.VMEM((8, 64, LANE), BF16),
            pltpu.VMEM((4, 16, LANE), F32),
            pltpu.VMEM((4, 16, LANE), BF16),
            pltpu.VMEM((4, 16, LANE), BF16),
            pltpu.VMEM((4, 16, LANE), BF16),
            pltpu.VMEM((4, 16, LANE), BF16),
            pltpu.VMEM((LANE, 256), F32),
            pltpu.VMEM((3 * LANE, 4 * LANE), BF16),
            pltpu.VMEM((3, LANE, 256), BF16),
            dma((4,)), dma((4,)),
            dma((8,)), dma((8,)), dma((8,)), dma((8,)), dma((8,)), dma((8,)),
            dma((2,)), dma((2,)), dma, dma,
            dma((4,)), dma((4,)), dma((8,)), dma((8,)), dma((8,)), dma((8,)), dma((4,)), dma((4,)),
            dma((4,)), dma((4,)),
        ],
        compiler_params=pltpu.CompilerParams(
            collective_id=0, has_side_effects=True, vmem_limit_bytes=60 * 1024 * 1024
        ),
        cost_estimate=pl.CostEstimate(
            flops=2 * 5 * TOK * D * HID, bytes_accessed=9 * 1024 * 1024, transcendentals=TOK * HID
        ),
    )(block_input, grad_out, ln_gain.reshape(1, D), w_in.T, w_out)
    grad_input, grad_w_in, grad_w_out = pl.pallas_call(
        place_outputs,
        out_shape=(
            jax.ShapeDtypeStruct((PIECE, TOK), BF16),
            jax.ShapeDtypeStruct((HID, QUART), F32),
            jax.ShapeDtypeStruct((HID, QUART), F32),
        ),
        in_specs=[pl.BlockSpec(memory_space=pl.ANY)] * 3,
        out_specs=[pl.BlockSpec(memory_space=pl.ANY)] * 3,
        scratch_shapes=[
            pltpu.VMEM((PIECE, TOK), BF16),
            pltpu.VMEM((2, HID, QUART), F32),
            dma((9,)),
            dma((9,)),
        ],
        compiler_params=pltpu.CompilerParams(vmem_limit_bytes=60 * 1024 * 1024),
    )(grad_input, grad_w_in, grad_w_out)
    return grad_input.T, grad_w_in.T, grad_w_out


def solution(mesh):
    in_specs = (P("dp", None), P("dp", None), P(), P(None, "mp"), P("mp", None))
    out_specs = (P("dp", "mp"), P("dp", "mp"), P("mp", "dp"))
    return jax.shard_map(shards, mesh=mesh, in_specs=in_specs, out_specs=out_specs, check_vma=False)
```

```python
import jax
import jax.numpy as jnp
from jax import lax
from jax.experimental import pallas as pl
from jax.experimental.pallas import tpu as pltpu
from jax.sharding import PartitionSpec as P

F32 = jnp.float32
BF16 = jnp.bfloat16
D = 6144
TOK = 192
HID = 96
LANE = 128
CCOL = D // 8
TPART = TOK // 4
ZCOL = CCOL // 8
PIECE = D // 256
QUART = D // 4
XROWS = 48


def contract_last(left, right):
    return lax.dot_general(left, right, (((1,), (1,)), ((), ())), preferred_element_type=F32)


def remote(src, dst, send, recv, dp, mp):
    return pltpu.make_async_remote_copy(
        src_ref=src,
        dst_ref=dst,
        send_sem=send,
        recv_sem=recv,
        device_id=(dp, mp),
        device_id_type=pl.DeviceIdType.MESH,
    )


def hi_lo(value):
    high = value.astype(BF16).astype(F32)
    return high, (value - high).astype(BF16).astype(F32)


def in_lanes(rows, first, one, two):
    lanes = lax.broadcasted_iota(jnp.int32, (rows, LANE), 1)
    result = jnp.zeros((rows, LANE), F32)
    for k, part in enumerate(hi_lo(one) + hi_lo(two)):
        result = jnp.where(lanes == first + k, part, result)
    return result


def pair_sums(parts):
    return parts[:, 0:1] + parts[:, 1:2], parts[:, 2:3] + parts[:, 3:4]


def kernel(
    x_hbm, go_hbm, gain_ref, win_hbm, wout_hbm,
    gi_ref, gwin_ref, gwout_ref,
    x_v, go_v, g_v, win_v, wout_v, wg, gpg, gain3, pre_s, ga_s, u_s, stat_s, tr_s, gp_t, act_t,
    pair_send, pair_recv, xh_send, xh_recv, gg_s, b_send, b_recv, c_own, c_send, c_recv,
    o_own, o_send, o_recv, t_own, t_send, t_recv, last_send, final, fin_t, fold, unfold,
    x_sem, load_sem, a_send, a_recv, f_send, f_recv, g_send, g_recv, p_send, p_recv,
    h_send, h_recv, bs_sem, br_sem, cs_sem, cr_sem, os_sem, or_sem, ts_sem, tr_sem, e_send, e_recv,
):
    dp = lax.axis_index("dp")
    mp = lax.axis_index("mp")
    xh, core = dp // 2, dp % 2
    z, xl, y = mp // 16, (mp // 8) % 2, mp % 8
    zh, zl, yh, yl = z // 2, z % 2, y // 2, y % 2
    cube = 4 * xl + 2 * yl + zl
    pair = 2 * xh + (1 - core)
    far = 2 * (1 - xh) + core

    def place(in_cube, on_y, on_z):
        zp = 2 * on_z + in_cube % 2
        return zp * 16 + (in_cube // 4) * 8 + 2 * on_y + (in_cube // 2) % 2

    def flip(d):
        return (
            4 * ((xl + d // 4) % 2) + 2 * ((yl + (d // 2) % 2) % 2) + (zl + d % 2) % 2
        )

    def cube_mp(d):
        return place(flip(d), yh, zh)

    def y_mp(d):
        return place(cube, (yh + d) % 4, zh)

    def z_mp(d):
        return place(cube, yh, (zh + d) % 8)

    def owner(k):
        return 32 * cube + 4 * zh + k

    def holder(k):
        return place(mp // 32, k, (mp % 32) // 4)

    own_owner = mp // 4 == 8 * cube + zh

    x_loads = [
        pltpu.make_async_copy(
            x_hbm.at[pl.ds(i * XROWS, XROWS)], x_v.at[pl.ds(i * XROWS, XROWS)], x_sem.at[i]
        )
        for i in range(TOK // XROWS)
    ]
    win_load = pltpu.make_async_copy(win_hbm, win_v.at[pl.ds(0, HID)], load_sem.at[0])
    wout_load = pltpu.make_async_copy(wout_hbm, wout_v.at[pl.ds(0, HID)], load_sem.at[1])
    go_load = pltpu.make_async_copy(go_hbm, go_v, load_sem.at[2])
    own_cols = pl.ds(pl.multiple_of(cube * CCOL, CCOL), CCOL)
    own_load = pltpu.make_async_copy(
        win_hbm.at[:, own_cols],
        wg.at[pl.ds(pl.multiple_of(cube * LANE, LANE), HID)],
        load_sem.at[3],
    )
    for load in x_loads:
        load.start()
    win_load.start()
    wout_load.start()
    go_load.start()
    own_load.start()

    barrier = pltpu.get_barrier_semaphore()

    def greet(to_dp, to_mp_):
        pl.semaphore_signal(
            barrier, inc=1, device_id=(to_dp, to_mp_), device_id_type=pl.DeviceIdType.MESH
        )

    @pl.loop(1, 8)
    def _(d):
        greet(dp, cube_mp(d))
        greet(dp, z_mp(d))

    @pl.loop(1, 4)
    def _(d):
        greet(dp, y_mp(d))

    greet(pair, mp)
    greet(far, mp)
    for k in range(4):

        @pl.when(owner(k) != mp)
        def _():
            greet(dp, owner(k))

        @pl.when(holder(k) != mp)
        def _():
            greet(dp, holder(k))

    pl.semaphore_wait(barrier, 7 + 7 + 3 + 2 + jnp.where(own_owner, 6, 8))

    def block_copy(d):
        return remote(
            win_hbm.at[pl.ds(pl.multiple_of(core * 48, 16), 48), pl.ds(pl.multiple_of(flip(d) * CCOL, CCOL), CCOL)],
            wg.at[pl.ds(pl.multiple_of(cube * LANE + core * 48, 16), 48)],
            a_send.at[d], a_recv.at[d], dp, cube_mp(d),
        )

    def landed(d, half):
        return wg.at[pl.ds(pl.multiple_of(flip(d) * LANE + half * 48, 16), 48)]

    def block_arrival(d):
        return remote(
            landed(d, core), landed(d, core), a_send.at[d], a_recv.at[d], dp, cube_mp(d)
        )

    def forward(d):
        return remote(landed(d, core), landed(d, core), f_send.at[d], f_recv.at[d], pair, mp)

    def forward_arrival(d):
        there = landed(d, 1 - core)
        return remote(there, there, f_send.at[d], f_recv.at[d], pair, mp)

    @pl.loop(1, 8)
    def _(d):
        block_copy(8 - d).start()

    win_v[HID:, :] = jnp.zeros((LANE - HID, D), BF16)
    wout_v[HID:, :] = jnp.zeros((LANE - HID, D), BF16)

    gain = gain_ref[...]
    g_hi = gain.astype(BF16).astype(F32)
    g_mid = (gain - g_hi).astype(BF16).astype(F32)
    g_low = gain - g_hi - g_mid
    row = lax.broadcasted_iota(jnp.int32, (16, D), 0)
    gain3[...] = jnp.where(
        row == 0, g_hi, jnp.where(row == 1, g_mid, jnp.where(row == 2, g_low, 0.0))
    ).astype(BF16)

    lane = lax.broadcasted_iota(jnp.int32, (16, LANE), 1)

    def norm_chunk(i):
        x_loads[i].wait()

        @pl.loop(0, XROWS // 16)
        def _(t):
            rows = pl.ds(pl.multiple_of(i * XROWS + t * 16, 16), 16)
            tile = x_v[rows, :].astype(F32)
            mean = jnp.sum(tile, axis=1, keepdims=True) * (1.0 / D)
            centred = tile - mean
            inv = lax.rsqrt(jnp.sum(centred * centred, axis=1, keepdims=True) * (1.0 / D) + 1e-06)
            g_v[rows, :] = (centred * inv * gain_ref[...]).astype(BF16)
            stat_s[rows, :] = jnp.where(lane < 64, mean, inv)

    norm_chunk(0)

    for i in range(1, TOK // XROWS):
        norm_chunk(i)

    win_load.wait()
    wout_load.wait()
    go_load.wait()
    pre_s[...] = jnp.zeros_like(pre_s)
    u_s[...] = jnp.zeros_like(u_s)
    ga_s[...] = jnp.zeros_like(ga_s)

    @pl.loop(0, 4)
    def _(k):
        part = pl.ds(pl.multiple_of(k * 1536, 1536), 1536)
        w_part = win_v[:, part]
        pre_s[...] += contract_last(g_v[:, part], w_part)
        u_s[...] += contract_last(gain3[:, part], w_part)
        ga_s[...] += contract_last(go_v[:, part], wout_v[:, part])

    pre = pre_s[...]
    cdf = 0.5 * (1.0 + lax.erf(pre * 0.7071067811865476))
    act = (pre * cdf).astype(BF16).astype(F32)
    slope = cdf + pre * jnp.exp(-0.5 * pre * pre) * 0.3989422804014327
    gp = (ga_s[...] * slope).astype(BF16).astype(F32)
    u_row = jnp.sum(u_s[...], axis=0, keepdims=True)
    sum_one = jnp.sum(gp * u_row, axis=1, keepdims=True)
    sum_two = jnp.sum(gp * pre, axis=1, keepdims=True)
    own_block = pl.ds(pl.multiple_of(cube * LANE, LANE), LANE)
    gpg[:, own_block] = (gp + in_lanes(TOK, HID, sum_one, sum_two)).astype(BF16)

    def gather_copy(d):
        mine = gpg.at[:, own_block]
        return remote(mine, mine, g_send.at[d], g_recv.at[d], dp, cube_mp(d))

    def gather_arrival(d):
        there = gpg.at[:, pl.ds(pl.multiple_of(flip(d) * LANE, LANE), LANE)]
        return remote(there, there, g_send.at[d], g_recv.at[d], dp, cube_mp(d))

    @pl.loop(1, 8)
    def _(d):
        gather_copy(8 - d).start()

    @pl.loop(1, 8)
    def _(d):
        block_arrival(8 - d).wait_recv()
        forward(8 - d).start()

    for i in range(8):
        wg[i * LANE + HID : (i + 1) * LANE, :] = jnp.zeros((LANE - HID, CCOL), BF16)

    tr_s[TOK:, :] = jnp.zeros((256 - TOK, LANE), F32)
    for values, target in ((gp, gp_t), (act, act_t)):
        tr_s[:TOK, :] = values
        for b in range(2):
            target[:, b * 128 : (b + 1) * 128] = tr_s[b * 128 : (b + 1) * 128, :].T.astype(BF16)
    sides = ((gp_t, g_v, gwin_ref), (act_t, go_v, gwout_ref))

    def product(side, quarter, t):
        left, right, _ = sides[side]
        cols = pl.ds(pl.multiple_of(quarter * QUART + t * 768, 128), 768)
        return jnp.dot(left[:HID, :TOK], right[:, cols], preferred_element_type=F32)

    def pair_copy(r):
        return remote(pair_send.at[r], pair_recv.at[r], p_send.at[r], p_recv.at[r], pair, mp)

    for r in range(2):
        half = 1 - xh if r == 0 else xh
        for side in range(2):
            for t in range(2):
                pair_send[r, side, :, t * 768 : (t + 1) * 768] = product(
                    side, 2 * half + 1 - core, t
                ).astype(BF16)
        pair_copy(r).start()

    for side in range(2):
        for t in range(2):
            sides[side][2][:, t * 768 : (t + 1) * 768] = product(side, dp, t)

    pair_copy(0).wait_recv()
    for side in range(2):
        for t in range(2):
            cols = slice(t * 768, (t + 1) * 768)
            xh_send[side, :, cols] = (
                product(side, far, t) + pair_recv[0, side, :, cols].astype(F32)
            ).astype(BF16)
    far_copy = remote(xh_send, xh_recv, h_send, h_recv, far, mp)
    far_copy.start()

    own_load.wait()

    @pl.loop(1, 8)
    def _(d):
        gather_arrival(d).wait_recv()
        forward_arrival(d).wait_recv()

    packed = jnp.zeros((TOK, LANE), F32)
    for i in range(8):
        packed += gpg[:, i * LANE : (i + 1) * LANE].astype(F32)
    gg_s[:, CCOL:] = in_lanes(TOK, 0, *pair_sums(packed[:, HID : HID + 4]))
    gg_s[:, :CCOL] = jnp.dot(gpg[...], wg[...], preferred_element_type=F32)

    far_first = (4, 3, 5, 2, 6, 1, 7)

    def pieces(values, own, send):
        rows = values.shape[0]
        lanes = lax.broadcasted_iota(jnp.int32, (rows, LANE), 1)
        tail = in_lanes(rows, ZCOL, *pair_sums(values[:, CCOL : CCOL + 4]))
        for k in range(8):
            piece = jnp.where(lanes < ZCOL, values[:, k * ZCOL : k * ZCOL + LANE], tail)
            own[k] = piece
            send[k] = piece.astype(BF16)

    def token_rows(d):
        return pl.ds(pl.multiple_of((yh + d) % 4 * 32, 32), 32)

    def token_copy(d):
        return remote(b_send.at[d], b_recv.at[d], bs_sem.at[d], br_sem.at[d], dp, y_mp(d))

    def column_copy(d):
        return remote(
            c_send.at[(zh + d) % 8], c_recv.at[d], cs_sem.at[d], cr_sem.at[d], dp, z_mp(d)
        )

    def other_column_copy(d):
        return remote(
            o_send.at[(zh + d) % 8], o_recv.at[d], os_sem.at[d], or_sem.at[d], dp, z_mp(d)
        )

    def other_token_copy(d):
        return remote(
            t_send.at[(yh + d) % 4], t_recv.at[d], ts_sem.at[d], tr_sem.at[d], dp, y_mp(d)
        )

    for d in (2, 1, 3):
        b_send[d] = gg_s[token_rows(d), :].astype(BF16)
        token_copy(d).start()
    pieces(gg_s[128:, :], o_own, o_send)
    for d in far_first:
        other_column_copy(d).start()

    from_lane = lax.broadcasted_iota(jnp.int32, (LANE, LANE), 0)
    to_lane = lax.broadcasted_iota(jnp.int32, (LANE, LANE), 1)
    for g in range(3):
        in_data = jnp.where(to_lane >= 32 * g, jnp.where(to_lane < 32 * g + PIECE, 1.0, 0.0), 0.0)
        in_tail = jnp.where(
            to_lane >= 32 * g + PIECE, jnp.where(to_lane < 32 * g + PIECE + 4, 1.0, 0.0), 0.0
        )
        tail_hit = jnp.where(from_lane == to_lane + (ZCOL - PIECE - 32 * g), in_tail, 0.0)
        for k in range(4):
            hit = jnp.where(from_lane == to_lane + (PIECE * k - 32 * g), in_data, 0.0) + tail_hit
            fold[g * LANE : (g + 1) * LANE, k * LANE : (k + 1) * LANE] = hit.astype(BF16)
    from_row = lax.broadcasted_iota(jnp.int32, (16, 256), 0)
    token = lax.broadcasted_iota(jnp.int32, (16, 256), 1)
    for g in range(3):
        unfold[g, 64:, :] = jnp.zeros((64, 256), BF16)
        for i in range(4):
            unfold[g, i * 16 : (i + 1) * 16, :] = jnp.where(
                token == from_row + (32 * i + 16 * g if g < 2 else 128 + 16 * i), 1.0, 0.0
            ).astype(BF16)

    part = gg_s[token_rows(0), :]
    for d in (1, 3, 2):
        token_copy(d).wait_recv()
        part += b_recv[d].astype(F32)
    pieces(part, c_own, c_send)
    for d in far_first:
        column_copy(d).start()

    o_sum = o_own[zh]
    for d in (1, 7, 2, 6, 3, 5, 4):
        other_column_copy(d).wait_recv()
        o_sum += o_recv[d].astype(F32)
    lanes = lax.broadcasted_iota(jnp.int32, (64, LANE), 1)
    tail = in_lanes(64, ZCOL, *pair_sums(o_sum[:, ZCOL : ZCOL + 4]))
    o_sum = jnp.where(lanes < ZCOL, o_sum, tail)
    for k in range(4):
        t_own[k] = o_sum[16 * k : 16 * (k + 1)]
        t_send[k] = t_own[k].astype(BF16)
    for d in (2, 1, 3):
        other_token_copy(d).start()

    c_sum = c_own[zh]
    for d in (1, 7, 2, 6, 3, 5, 4):
        column_copy(d).wait_recv()
        c_sum += c_recv[d].astype(F32)
    t_sum = t_own[yh]
    for d in (1, 3, 2):
        other_token_copy(d).wait_recv()
        t_sum += t_recv[d].astype(F32)

    lanes = lax.broadcasted_iota(jnp.int32, (TPART, LANE), 1)
    summed = jnp.concatenate([c_sum, t_sum], axis=0)
    tail = in_lanes(TPART, ZCOL, *pair_sums(summed[:, ZCOL : ZCOL + 4]))
    rounded = jnp.where(lanes < ZCOL, summed, tail).astype(BF16)
    folded = jnp.dot(
        jnp.concatenate([rounded[16 * g : 16 * (g + 1)] for g in range(3)], axis=1),
        fold[...],
        preferred_element_type=F32,
    ).astype(BF16)
    for k in range(4):
        last_send[k] = folded[:, k * LANE : (k + 1) * LANE]

    def last_copy(k):
        return remote(
            last_send.at[k], final.at[yh], e_send.at[k], e_recv.at[yh], dp, owner(k)
        )

    def last_arrival(k):
        return remote(final.at[k], final.at[k], e_send.at[k], e_recv.at[k], dp, holder(k))

    for k in range(4):

        @pl.when(owner(k) != mp)
        def _():
            last_copy(k).start()

    @pl.when(own_owner)
    def _():
        final[yh] = last_send[mp % 4]

    pair_copy(1).wait_recv()
    far_copy.wait_recv()
    for side in range(2):
        out = sides[side][2]
        out[...] += pair_recv[1, side].astype(F32) + xh_recv[side].astype(F32)

    base = pl.multiple_of(jnp.minimum((mp * PIECE) // 128 * 128, D - 256), 128)
    off = mp * PIECE - base
    span = pl.ds(base, 256)
    picks = lax.broadcasted_iota(jnp.int32, (32, 256), 1) == (
        lax.broadcasted_iota(jnp.int32, (32, 256), 0) + off
    )
    pick = jnp.where(picks, 1.0, 0.0)
    x_t = contract_last(pick.astype(BF16), x_v[:, span])[:PIECE]
    go_t = contract_last(pick.astype(BF16), go_v[:, span])[:PIECE]
    gain_t = jnp.sum(pick * gain_ref[:, span], axis=1, keepdims=True)[:PIECE]
    stat_s[TOK:, :] = jnp.zeros((256 - TOK, LANE), F32)
    for b in range(2):
        fin_t[:, b * 128 : (b + 1) * 128] = stat_s[b * 128 : (b + 1) * 128, :].T
    mean_row, inv_row = fin_t[0:1, :TOK], fin_t[64:65, :TOK]
    normed = (x_t - mean_row) * inv_row

    for k in range(4):

        @pl.when(holder(k) != mp)
        def _():
            last_arrival(k).wait_recv()

    tr_s[64:128, :] = jnp.zeros((64, LANE), F32)
    for i in range(4):
        tr_s[i * 16 : (i + 1) * 16, :] = final[i].astype(F32)
    turned = tr_s[:128, :].T.astype(BF16)
    laid = jnp.zeros((32, 256), F32)
    for g in range(3):
        laid += jnp.dot(turned[32 * g : 32 * (g + 1)], unfold[g], preferred_element_type=F32)
    laid = laid[:, :TOK]
    grad_normed = laid[:PIECE] * gain_t
    mean_one = (laid[PIECE : PIECE + 1] + laid[PIECE + 1 : PIECE + 2]) * (1.0 / D)
    mean_two = (laid[PIECE + 2 : PIECE + 3] + laid[PIECE + 3 : PIECE + 4]) * (1.0 / D)
    gi_ref[...] = (go_t + inv_row * (grad_normed - mean_one - normed * mean_two)).astype(BF16)

    @pl.loop(1, 8)
    def _(d):
        block_copy(d).wait_send()
        forward(d).wait_send()
        gather_copy(d).wait_send()
        column_copy(d).wait_send()
        other_column_copy(d).wait_send()

    for r in range(2):
        pair_copy(r).wait_send()
    far_copy.wait_send()

    @pl.loop(1, 4)
    def _(d):
        token_copy(d).wait_send()
        other_token_copy(d).wait_send()

    for k in range(4):

        @pl.when(owner(k) != mp)
        def _():
            last_copy(k).wait_send()


def place_outputs(gi, gwin, gwout, gi_out, gwin_out, gwout_out, gi_v, w_v, in_sem, out_sem):
    parts = [(gi, gi_v, gi_out)]
    for side, (array, out) in enumerate(((gwin, gwin_out), (gwout, gwout_out))):
        for k in range(4):
            rows = pl.ds(k * 24, 24)
            parts.append((array.at[rows], w_v.at[side, rows], out.at[rows]))
    reads, writes = [], []
    for k, (array, held, out) in enumerate(parts):
        reads.append(pltpu.make_async_copy(array, held, in_sem.at[k]))
        writes.append(pltpu.make_async_copy(held, out, out_sem.at[k]))
    for read in reads:
        read.start()
    for read, write in zip(reads, writes):
        read.wait()
        write.start()
    for write in writes:
        write.wait()


def shards(block_input, grad_out, ln_gain, w_in, w_out):
    dma = pltpu.SemaphoreType.DMA
    grad_input, grad_w_in, grad_w_out = pl.pallas_call(
        kernel,
        out_shape=(
            jax.ShapeDtypeStruct((PIECE, TOK), BF16),
            jax.ShapeDtypeStruct((HID, QUART), F32),
            jax.ShapeDtypeStruct((HID, QUART), F32),
        ),
        in_specs=[
            pl.BlockSpec(memory_space=pl.ANY),
            pl.BlockSpec(memory_space=pl.ANY),
            pl.BlockSpec(memory_space=pltpu.VMEM),
            pl.BlockSpec(memory_space=pl.ANY),
            pl.BlockSpec(memory_space=pl.ANY),
        ],
        out_specs=[pl.BlockSpec(memory_space=pltpu.VMEM)] * 3,
        scratch_shapes=[
            pltpu.VMEM((TOK, D), BF16),
            pltpu.VMEM((TOK, D), BF16),
            pltpu.VMEM((TOK, D), BF16),
            pltpu.VMEM((LANE, D), BF16),
            pltpu.VMEM((LANE, D), BF16),
            pltpu.VMEM((8 * LANE, CCOL), BF16),
            pltpu.VMEM((TOK, 8 * LANE), BF16),
            pltpu.VMEM((16, D), BF16),
            pltpu.VMEM((TOK, LANE), F32),
            pltpu.VMEM((TOK, LANE), F32),
            pltpu.VMEM((16, LANE), F32),
            pltpu.VMEM((256, LANE), F32),
            pltpu.VMEM((256, LANE), F32),
            pltpu.VMEM((LANE, 256), BF16),
            pltpu.VMEM((LANE, 256), BF16),
            pltpu.VMEM((2, 2, HID, QUART), BF16),
            pltpu.VMEM((2, 2, HID, QUART), BF16),
            pltpu.VMEM((2, HID, QUART), BF16),
            pltpu.VMEM((2, HID, QUART), BF16),
            pltpu.VMEM((TOK, CCOL + LANE), F32),
            pltpu.VMEM((4, 32, CCOL + LANE), BF16),
            pltpu.VMEM((4, 32, CCOL + LANE), BF16),
            pltpu.VMEM((8, 32, LANE), F32),
            pltpu.VMEM((8, 32, LANE), BF16),
            pltpu.VMEM((8, 32, LANE), BF16),
            pltpu.VMEM((8, 64, LANE), F32),
            pltpu.VMEM((8, 64, LANE), BF16),
            pltpu.VMEM((8, 64, LANE), BF16),
            pltpu.VMEM((4, 16, LANE), F32),
            pltpu.VMEM((4, 16, LANE), BF16),
            pltpu.VMEM((4, 16, LANE), BF16),
            pltpu.VMEM((4, 16, LANE), BF16),
            pltpu.VMEM((4, 16, LANE), BF16),
            pltpu.VMEM((LANE, 256), F32),
            pltpu.VMEM((3 * LANE, 4 * LANE), BF16),
            pltpu.VMEM((3, LANE, 256), BF16),
            dma((4,)), dma((4,)),
            dma((8,)), dma((8,)), dma((8,)), dma((8,)), dma((8,)), dma((8,)),
            dma((2,)), dma((2,)), dma, dma,
            dma((4,)), dma((4,)), dma((8,)), dma((8,)), dma((8,)), dma((8,)), dma((4,)), dma((4,)),
            dma((4,)), dma((4,)),
        ],
        compiler_params=pltpu.CompilerParams(
            collective_id=0, has_side_effects=True, vmem_limit_bytes=60 * 1024 * 1024
        ),
        cost_estimate=pl.CostEstimate(
            flops=2 * 5 * TOK * D * HID, bytes_accessed=9 * 1024 * 1024, transcendentals=TOK * HID
        ),
    )(block_input, grad_out, ln_gain.reshape(1, D), w_in.T, w_out)
    grad_input, grad_w_in, grad_w_out = pl.pallas_call(
        place_outputs,
        out_shape=(
            jax.ShapeDtypeStruct((PIECE, TOK), BF16),
            jax.ShapeDtypeStruct((HID, QUART), F32),
            jax.ShapeDtypeStruct((HID, QUART), F32),
        ),
        in_specs=[pl.BlockSpec(memory_space=pl.ANY)] * 3,
        out_specs=[pl.BlockSpec(memory_space=pl.ANY)] * 3,
        scratch_shapes=[
            pltpu.VMEM((PIECE, TOK), BF16),
            pltpu.VMEM((2, HID, QUART), F32),
            dma((9,)),
            dma((9,)),
        ],
        compiler_params=pltpu.CompilerParams(vmem_limit_bytes=60 * 1024 * 1024),
    )(grad_input, grad_w_in, grad_w_out)
    return grad_input.T, grad_w_in.T, grad_w_out


def solution(mesh):
    in_specs = (P("dp", None), P("dp", None), P(), P(None, "mp"), P("mp", None))
    out_specs = (P("dp", "mp"), P("dp", "mp"), P("mp", "dp"))
    return jax.shard_map(shards, mesh=mesh, in_specs=in_specs, out_specs=out_specs, check_vma=False)
```
